32 devices in a mesh: dp: 8 (over z, y), mp: 4 (over x, core).
Axes of the slice: x: 2, y: 2, z: 4, core: 2. Of those that a mesh axis runs over, the one named last changes fastest.
Arguments:
- block_in: float32 [4096, 1152], P('dp'), may hold values from -6 to 6
- out_grad: float32 [4096, 1152], P('dp'), may hold values from -6 to 6
- segment_ids: int32 [4096], replicated, may hold values from 0 to 3, never falling along the last dimension, each value on 1 to 2048 neighbouring positions
- w_query: float32 [1152, 1024], P('dp', 'mp'), may hold values from -0.1875 to 0.1875
- w_keyval: float32 [1152, 512], P(('dp', 'mp')), may hold values from -0.1875 to 0.1875
- w_out: float32 [1024, 1152], P('mp', 'dp'), may hold values from -0.1875 to 0.1875
- w_gateup: float32 [2, 1152, 6912], P(None, 'dp', 'mp'), may hold values from -0.1875 to 0.1875
- w_down: float32 [6912, 1152], P('mp', 'dp'), may hold values from -0.078125 to 0.078125
- gain_layers: float32 [4, 1152], P(None, ('dp', 'mp')), may hold values from -0.04 to 0.04
- gain_heads: float32 [2, 256], P(None, ('dp', 'mp')), may hold values from -0.04 to 0.04
- mom_query: float32 [1152, 1024], P('dp', 'mp'), may hold values from -0.18 to 0.18
- var_query: float32 [1152, 1024], P('dp', 'mp'), may hold values from 0.025 to 0.1
- mom_keyval: float32 [1152, 512], P(('dp', 'mp')), may hold values from -0.18 to 0.18
- var_keyval: float32 [1152, 512], P(('dp', 'mp')), may hold values from 0.02 to 4
- mom_out: float32 [1024, 1152], P('mp', 'dp'), may hold values from -0.18 to 0.18
- var_out: float32 [1024, 1152], P('mp', 'dp'), may hold values from 0.025 to 0.1
- mom_gateup: float32 [2, 1152, 6912], P(None, 'dp', 'mp'), may hold values from -0.18 to 0.18
- var_gateup: float32 [2, 1152, 6912], P(None, 'dp', 'mp'), may hold values from 0.025 to 0.1
- mom_down: float32 [6912, 1152], P('mp', 'dp'), may hold values from -0.18 to 0.18
- var_down: float32 [6912, 1152], P('mp', 'dp'), may hold values from 0.025 to 0.1
- mom_layers: float32 [4, 1152], P(None, ('dp', 'mp')), may hold values from -0.18 to 0.18
- var_layers: float32 [4, 1152], P(None, ('dp', 'mp')), may hold values from 0.025 to 0.1
- mom_heads: float32 [2, 256], P(None, ('dp', 'mp')), may hold values from -0.18 to 0.18
- var_heads: float32 [2, 256], P(None, ('dp', 'mp')), may hold values from 0.02 to 4
Outputs:
- block_out: float32 [4096, 1152], P('dp')
- grad_input: float32 [4096, 1152], P('dp')
- grad_query: float32 [1152, 1024], P('dp', 'mp')
- grad_keyval: float32 [1152, 512], P(('dp', 'mp'))
- grad_out: float32 [1024, 1152], P('mp', 'dp')
- grad_gateup: float32 [2, 1152, 6912], P(None, 'dp', 'mp')
- grad_down: float32 [6912, 1152], P('mp', 'dp')
- grad_layers: float32 [4, 1152], P(None, ('dp', 'mp'))
- grad_heads: float32 [2, 256], P(None, ('dp', 'mp'))
- fresh_query: float32 [1152, 1024], P('dp', 'mp')
- fresh_keyval: float32 [1152, 512], P(('dp', 'mp'))
- fresh_out: float32 [1024, 1152], P('mp', 'dp')
- fresh_gateup: float32 [2, 1152, 6912], P(None, 'dp', 'mp')
- fresh_down: float32 [6912, 1152], P('mp', 'dp')
- fresh_layers: float32 [4, 1152], P(None, ('dp', 'mp'))
- fresh_heads: float32 [2, 256], P(None, ('dp', 'mp'))
- fresh_mom_query: float32 [1152, 1024], P('dp', 'mp')
- fresh_mom_keyval: float32 [1152, 512], P(('dp', 'mp'))
- fresh_mom_out: float32 [1024, 1152], P('mp', 'dp')
- fresh_mom_gateup: float32 [2, 1152, 6912], P(None, 'dp', 'mp')
- fresh_mom_down: float32 [6912, 1152], P('mp', 'dp')
- fresh_mom_layers: float32 [4, 1152], P(None, ('dp', 'mp'))
- fresh_mom_heads: float32 [2, 256], P(None, ('dp', 'mp'))
- fresh_var_query: float32 [1152, 1024], P('dp', 'mp')
- fresh_var_keyval: float32 [1152, 512], P(('dp', 'mp'))
- fresh_var_out: float32 [1024, 1152], P('mp', 'dp')
- fresh_var_gateup: float32 [2, 1152, 6912], P(None, 'dp', 'mp')
- fresh_var_down: float32 [6912, 1152], P('mp', 'dp')
- fresh_var_layers: float32 [4, 1152], P(None, ('dp', 'mp'))
- fresh_var_heads: float32 [2, 256], P(None, ('dp', 'mp'))
The draws below stay inside these ranges and needn't reach their ends.
Inputs may be any that keep to these rules, and one draw needn't show every extreme that they name: `segment_ids`: document ids, never falling along the tokens; a document has 2048 tokens or fewer.
All inputs are finite; a program needn't handle non-finite values.
Results may differ from the reference program's by a relative error of at most 0.025.
Values may be sent and summed in bfloat16 or wider, within the bound.
No kernel may reach another device: no remote copies, remote signals or barrier semaphores. Data moves between devices by JAX's collectives and lax.ppermute only.
A program may use at most 192 MiB of HBM per device.

```python
import math
import jax
import jax.numpy as jnp
import numpy as np
from jax import lax

D = 1152
HEADS = 4
HD = 256
FF = 6912
SEQ = 2048
ADAM_STEP = 4
TOKENS = 4096


def levels(key, dims, cuts, low, top_value):
    gain, own = 1.0, jax.random.fold_in(key, 6)
    for dim, shards_of in cuts:
        heights = jnp.exp(jax.random.uniform(jax.random.fold_in(own, dim), (shards_of,), jnp.float32, low / len(cuts), top_value / len(cuts)))
        gain = gain * jnp.repeat(heights, dims[dim] // shards_of).reshape([-1 if axis == dim else 1 for axis in range(len(dims))])
    return gain


def length_profile(amount, total, most, skew):
    loads = [(1 << 20) // math.isqrt(standing ** skew) + 1 for standing in range(2, amount + 1)]
    spare, given = total - most - (amount - 1), [1] * (amount - 1)
    while spare > 0:
        candidates = [i for i in range(amount - 1) if given[i] < most]
        whole, budget = sum([loads[i] for i in candidates]), spare
        for i in candidates:
            extra = min(most - given[i], max(1, budget * loads[i] // whole), spare)
            given[i] = given[i] + extra
            spare = spare - extra
    return np.array([most] + given)


def ragged_sizes(own_key, number_of, total, limit, skew):
    if number_of == 2:
        one = jax.random.randint(own_key, (), max(1, total - limit), min(limit, total - 1) + 1)
        return jnp.stack([one, total - one])
    sizes = jnp.asarray(length_profile(number_of, total, limit, skew), jnp.int32)
    pairs = (number_of - 1) // 2
    donor, taker = sizes[1:1 + 2 * pairs:2], sizes[2:2 + 2 * pairs:2]
    slack = jnp.minimum(donor - 1, limit - taker)
    passed = jax.random.randint(jax.random.fold_in(own_key, 1), (pairs,), 0, 1 << 20) % (slack + 1)
    sizes = sizes.at[1:1 + 2 * pairs:2].set(donor - passed).at[2:2 + 2 * pairs:2].set(taker + passed)
    return sizes[jax.random.permutation(jax.random.fold_in(own_key, 2), number_of)]


def centred(key, extent, spread, bound, pieces=(), held_as=jnp.bfloat16):
    loudness = levels(key, extent, pieces, -0.22, 0.18) if pieces else 1.0
    drawn = jax.random.normal(key, extent, jnp.float32) * spread * loudness
    return jnp.minimum(jnp.maximum(drawn, -bound), bound).astype(held_as)


def setup_inputs(seed: int = 0) -> dict:
    key_list = jax.random.split(jax.random.key(seed), 25)
    block_in = centred(key_list[0], (TOKENS, D), 1.0, 6.0, ((0, 8),), jnp.float32)
    out_grad = centred(key_list[1], (TOKENS, D), 1.0, 6.0, ((0, 8),), jnp.float32)
    segment_ids = jnp.searchsorted(jnp.cumsum(ragged_sizes(key_list[2], 2 * TOKENS // SEQ, TOKENS, SEQ, 0)), jnp.arange(TOKENS), side="right").astype(jnp.int32)
    w_query = centred(key_list[3], (D, HEADS * HD), D ** -0.5, 0.1875, ((0, 8), (1, 4)), jnp.float32)
    w_keyval = centred(key_list[4], (D, 2 * HD), D ** -0.5, 0.1875, ((0, 32),), jnp.float32)
    w_out = centred(key_list[5], (HEADS * HD, D), (HEADS * HD) ** -0.5, 0.1875, ((0, 4), (1, 8)), jnp.float32)
    w_gateup = centred(key_list[6], (2, D, FF), D ** -0.5, 0.1875, ((1, 8), (2, 4)), jnp.float32)
    w_down = centred(key_list[7], (FF, D), FF ** -0.5, 0.078125, ((0, 4), (1, 8)), jnp.float32)
    gain_layers = centred(key_list[8], (4, D), 0.015, 0.04, ((1, 32),), jnp.float32)
    gain_heads = centred(key_list[9], (2, HD), 0.015, 0.04, ((1, 32),), jnp.float32)
    mom_query = centred(key_list[10], (D, HEADS * HD), 0.03, 0.18, ((0, 8), (1, 4)), jnp.float32)
    var_query = jnp.clip(jnp.exp(math.log(0.1) - 1.3862944 * jax.random.uniform(key_list[11], (D, HEADS * HD), jnp.float32) ** levels(key_list[11], (D, HEADS * HD), ((0, 8), (1, 4)), -0.2, 0.2)), 0.025, 0.1)
    mom_keyval = centred(key_list[12], (D, 2 * HD), 0.03, 0.18, ((0, 32),), jnp.float32)
    var_keyval = jnp.clip(jnp.exp(math.log(4.0) - 5.2983174 * jax.random.uniform(key_list[13], (D, 2 * HD), jnp.float32) ** levels(key_list[13], (D, 2 * HD), ((0, 32),), -0.2, 0.2)), 0.02, 4.0)
    mom_out = centred(key_list[14], (HEADS * HD, D), 0.03, 0.18, ((0, 4), (1, 8)), jnp.float32)
    var_out = jnp.clip(jnp.exp(math.log(0.1) - 1.3862944 * jax.random.uniform(key_list[15], (HEADS * HD, D), jnp.float32) ** levels(key_list[15], (HEADS * HD, D), ((0, 4), (1, 8)), -0.2, 0.2)), 0.025, 0.1)
    mom_gateup = centred(key_list[16], (2, D, FF), 0.03, 0.18, ((1, 8), (2, 4)), jnp.float32)
    var_gateup = jnp.clip(jnp.exp(math.log(0.1) - 1.3862944 * jax.random.uniform(key_list[17], (2, D, FF), jnp.float32) ** levels(key_list[17], (2, D, FF), ((1, 8), (2, 4)), -0.2, 0.2)), 0.025, 0.1)
    mom_down = centred(key_list[18], (FF, D), 0.03, 0.18, ((0, 4), (1, 8)), jnp.float32)
    var_down = jnp.clip(jnp.exp(math.log(0.1) - 1.3862944 * jax.random.uniform(key_list[19], (FF, D), jnp.float32) ** levels(key_list[19], (FF, D), ((0, 4), (1, 8)), -0.2, 0.2)), 0.025, 0.1)
    mom_layers = centred(key_list[20], (4, D), 0.03, 0.18, ((1, 32),), jnp.float32)
    var_layers = jnp.clip(jnp.exp(math.log(0.1) - 1.3862944 * jax.random.uniform(key_list[21], (4, D), jnp.float32) ** levels(key_list[21], (4, D), ((1, 32),), -0.2, 0.2)), 0.025, 0.1)
    mom_heads = centred(key_list[22], (2, HD), 0.03, 0.18, ((1, 32),), jnp.float32)
    var_heads = jnp.clip(jnp.exp(math.log(4.0) - 5.2983174 * jax.random.uniform(key_list[23], (2, HD), jnp.float32) ** levels(key_list[23], (2, HD), ((1, 32),), -0.2, 0.2)), 0.02, 4.0)
    return dict(block_in=block_in, out_grad=out_grad, segment_ids=segment_ids, w_query=w_query, w_keyval=w_keyval, w_out=w_out, w_gateup=w_gateup, w_down=w_down, gain_layers=gain_layers, gain_heads=gain_heads, mom_query=mom_query, var_query=var_query, mom_keyval=mom_keyval, var_keyval=var_keyval, mom_out=mom_out, var_out=var_out, mom_gateup=mom_gateup, var_gateup=var_gateup, mom_down=mom_down, var_down=var_down, mom_layers=mom_layers, var_layers=var_layers, mom_heads=mom_heads, var_heads=var_heads)


EPS = 1e-06
THETA = 1000000.0
LEARN = 0.02
BETA_ONE = 0.9
BETA_TWO = 0.95
ADAM_EPS = 1e-08
DECAY = 0.1
GELU_COEF = 0.7978845608028654
GELU_CUBE = 0.044715
NEG_FILL = -1e+30

def rms_scale(values):
    return lax.rsqrt(lax.optimization_barrier(jnp.mean(values * values, axis=-1, keepdims=True)) + EPS)

def norm_back(values, scale, factor, incoming):
    scaled = incoming * factor
    return scale * (scaled - values * (scale * scale) * lax.optimization_barrier(jnp.mean(scaled * values, axis=-1, keepdims=True)))

def rotate_half(values):
    middle = values.shape[-1] // 2
    return jnp.concatenate([-values[..., middle:], values[..., :middle]], axis=-1)

def rope_tables(position, width):
    middle = width // 2
    freqs = THETA ** (-2.0 * jnp.arange(middle, dtype=jnp.float32) / width)
    angle = position.astype(jnp.float32)[:, None] * freqs[None, :]
    cosine = jnp.concatenate([jnp.cos(angle), jnp.cos(angle)], axis=-1)
    sine = jnp.concatenate([jnp.sin(angle), jnp.sin(angle)], axis=-1)
    return (cosine, sine)

def gelu_parts(values):
    inner = GELU_COEF * (values + GELU_CUBE * values * values * values)
    tanh_val = jnp.tanh(inner)
    value = 0.5 * values * (1.0 + tanh_val)
    slope = 0.5 * (1.0 + tanh_val) + 0.5 * values * (1.0 - tanh_val * tanh_val) * GELU_COEF * (1.0 + 3.0 * GELU_CUBE * values * values)
    return (value, slope)

def adam_update(weight, mom, var, grad, decay):
    mom_new = BETA_ONE * mom + (1.0 - BETA_ONE) * grad
    var_new = BETA_TWO * var + (1.0 - BETA_TWO) * grad * grad
    fix_one = 1.0 - BETA_ONE ** ADAM_STEP
    fix_two = 1.0 - BETA_TWO ** ADAM_STEP
    direction = mom_new / fix_one / (jnp.sqrt(var_new / fix_two) + ADAM_EPS)
    return (weight - LEARN * (direction + decay * weight), mom_new, var_new)

def sequence_pass(weights, block_in, out_grad, segments):
    low_query, low_keyval, low_out, low_gateup, low_down, gain_scale, head_scale = weights
    bf = jnp.bfloat16
    fl = jnp.float32
    length = block_in.shape[0]
    width = HD
    heads = low_query.shape[1] // width
    factor = width ** (-0.5)
    position = jnp.arange(length, dtype=jnp.int32)
    cosine, sine = rope_tables(position, width)
    allowed = (position[None, :] <= position[:, None]) & (segments[None, :] == segments[:, None])
    scale_in = rms_scale(block_in)
    normed_in = (block_in * scale_in * gain_scale[0]).astype(bf)
    query_raw = jnp.dot(normed_in, low_query, preferred_element_type=fl).reshape(length, heads, width)
    keyval_raw = jnp.dot(normed_in, low_keyval, preferred_element_type=fl)
    key_raw = keyval_raw[:, :width]
    value_rows = keyval_raw[:, width:].astype(bf)
    scale_query = rms_scale(query_raw)
    query_norm = query_raw * scale_query * head_scale[0]
    query_rot = (query_norm * cosine[:, None, :] + rotate_half(query_norm) * sine[:, None, :]).astype(bf)
    scale_key = rms_scale(key_raw)
    key_norm = key_raw * scale_key * head_scale[1]
    key_rot = (key_norm * cosine + rotate_half(key_norm) * sine).astype(bf)
    scores = jnp.einsum('qhd,kd->hqk', query_rot.astype(fl), key_rot.astype(fl)) * factor
    masked = jnp.where(allowed[None], scores, NEG_FILL)
    top = lax.optimization_barrier(jnp.max(masked, axis=-1, keepdims=True))
    log_total = top + jnp.log(lax.optimization_barrier(jnp.sum(jnp.exp(masked - top), axis=-1, keepdims=True)))
    probs = jnp.exp(masked - log_total)
    probs_low = probs.astype(bf)
    attended = jnp.einsum('hqk,kd->qhd', probs_low.astype(fl), value_rows.astype(fl)).astype(bf).reshape(length, heads * width)
    attn_proj = jnp.dot(attended, low_out, preferred_element_type=fl)
    scale_attn = rms_scale(attn_proj)
    resid = block_in + attn_proj * scale_attn * gain_scale[1]
    scale_mid = rms_scale(resid)
    normed_mid = (resid * scale_mid * gain_scale[2]).astype(bf)
    gate_raw = jnp.dot(normed_mid, low_gateup[0], preferred_element_type=fl)
    up_raw = jnp.dot(normed_mid, low_gateup[1], preferred_element_type=fl)
    gelu_value, gelu_slope = gelu_parts(gate_raw)
    hidden = (gelu_value * up_raw).astype(bf)
    ffn_proj = jnp.dot(hidden, low_down, preferred_element_type=fl)
    scale_ffn = rms_scale(ffn_proj)
    block_out = resid + ffn_proj * scale_ffn * gain_scale[3]
    grad_ffn = norm_back(ffn_proj, scale_ffn, gain_scale[3], out_grad).astype(bf)
    grad_down = jnp.dot(hidden.T, grad_ffn, preferred_element_type=fl)
    grad_hidden = jnp.dot(grad_ffn, low_down.T, preferred_element_type=fl)
    grad_gate = (grad_hidden * up_raw * gelu_slope).astype(bf)
    grad_up = (grad_hidden * gelu_value).astype(bf)
    grad_gateup = jnp.stack([jnp.dot(normed_mid.T, grad_gate, preferred_element_type=fl), jnp.dot(normed_mid.T, grad_up, preferred_element_type=fl)])
    grad_mid = jnp.dot(grad_gate, low_gateup[0].T, preferred_element_type=fl) + jnp.dot(grad_up, low_gateup[1].T, preferred_element_type=fl)
    grad_resid = out_grad + norm_back(resid, scale_mid, gain_scale[2], grad_mid)
    grad_attn = norm_back(attn_proj, scale_attn, gain_scale[1], grad_resid).astype(bf)
    grad_out = jnp.dot(attended.T, grad_attn, preferred_element_type=fl)
    grad_attended = jnp.dot(grad_attn, low_out.T, preferred_element_type=fl).astype(bf).reshape(length, heads, width)
    row_delta = lax.optimization_barrier(jnp.sum(grad_attended.astype(fl) * attended.reshape(length, heads, width).astype(fl), axis=-1))
    grad_probs = jnp.einsum('qhd,kd->hqk', grad_attended.astype(fl), value_rows.astype(fl))
    grad_scores = (probs * (grad_probs - row_delta.T[:, :, None]) * factor).astype(bf)
    grad_qrot = jnp.einsum('hqk,kd->qhd', grad_scores.astype(fl), key_rot.astype(fl))
    grad_krot = jnp.einsum('hqk,qhd->kd', grad_scores.astype(fl), query_rot.astype(fl))
    grad_values = jnp.einsum('hqk,qhd->kd', probs_low.astype(fl), grad_attended.astype(fl))
    query_back = grad_qrot * cosine[:, None, :] - rotate_half(grad_qrot * sine[:, None, :])
    key_back = grad_krot * cosine - rotate_half(grad_krot * sine)
    grad_qin = norm_back(query_raw, scale_query, head_scale[0], query_back).astype(bf).reshape(length, heads * width)
    grad_kin = norm_back(key_raw, scale_key, head_scale[1], key_back)
    grad_kvin = jnp.concatenate([grad_kin, grad_values], axis=1).astype(bf)
    grad_query = jnp.dot(normed_in.T, grad_qin, preferred_element_type=fl)
    grad_keyval = jnp.dot(normed_in.T, grad_kvin, preferred_element_type=fl)
    grad_normed = jnp.dot(grad_qin, low_query.T, preferred_element_type=fl) + jnp.dot(grad_kvin, low_keyval.T, preferred_element_type=fl)
    grad_input = grad_resid + norm_back(block_in, scale_in, gain_scale[0], grad_normed)
    grad_layers = jnp.stack([lax.optimization_barrier(jnp.sum(grad_normed * block_in * scale_in, axis=0)), lax.optimization_barrier(jnp.sum(grad_resid * attn_proj * scale_attn, axis=0)), lax.optimization_barrier(jnp.sum(grad_mid * resid * scale_mid, axis=0)), lax.optimization_barrier(jnp.sum(out_grad * ffn_proj * scale_ffn, axis=0))])
    grad_heads = jnp.stack([lax.optimization_barrier(jnp.sum(query_back * query_raw * scale_query, axis=(0, 1))), lax.optimization_barrier(jnp.sum(key_back * key_raw * scale_key, axis=0))])
    grads = (grad_query, grad_keyval, grad_out, grad_gateup, grad_down, grad_layers, grad_heads)
    return ((block_out, grad_input), grads)

def reference(block_in, out_grad, segment_ids, w_query, w_keyval, w_out, w_gateup, w_down, gain_layers, gain_heads, mom_query, var_query, mom_keyval, var_keyval, mom_out, var_out, mom_gateup, var_gateup, mom_down, var_down, mom_layers, var_layers, mom_heads, var_heads):
    bf = jnp.bfloat16
    fl = jnp.float32
    gain_scale = 1.0 + lax.optimization_barrier(gain_layers.astype(bf)).astype(fl)
    head_scale = 1.0 + lax.optimization_barrier(gain_heads.astype(bf)).astype(fl)
    weights = (w_query.astype(bf), w_keyval.astype(bf), w_out.astype(bf), w_gateup.astype(bf), w_down.astype(bf), gain_scale, head_scale)
    masters = (w_query, w_keyval, w_out, w_gateup, w_down, gain_layers, gain_heads)
    margin = SEQ // 2
    total_rows = block_in.shape[0]
    padded_in = jnp.pad(block_in, ((margin, margin), (0, 0)))
    padded_grad = jnp.pad(out_grad, ((margin, margin), (0, 0)))
    padded_seg = jnp.pad(segment_ids, (margin, margin), constant_values=-1).astype(jnp.int32)
    count = (total_rows + SEQ) // SEQ

    def step(carry, inputs):
        rows_in, rows_grad, rows_seg = inputs
        outputs, grads = sequence_pass(weights, rows_in, rows_grad, rows_seg)
        return (tuple((total + piece for total, piece in zip(carry, grads))), outputs)
    zeros = tuple((jnp.zeros(master.shape, fl) for master in masters))
    sums, outputs = lax.scan(step, zeros, (padded_in.reshape(count, SEQ, -1), padded_grad.reshape(count, SEQ, -1), padded_seg.reshape(count, SEQ)))
    norm_factor = float(total_rows) ** (-0.5)
    totals = tuple((item * norm_factor for item in sums))
    block_out = outputs[0].reshape(count * SEQ, -1)[margin:margin + total_rows]
    grad_input = outputs[1].reshape(count * SEQ, -1)[margin:margin + total_rows]
    moms = (mom_query, mom_keyval, mom_out, mom_gateup, mom_down, mom_layers, mom_heads)
    varis = (var_query, var_keyval, var_out, var_gateup, var_down, var_layers, var_heads)
    decays = (DECAY, DECAY, DECAY, DECAY, DECAY, 0.0, 0.0)
    updated = [adam_update(master, mom, var, grad, decay) for master, mom, var, grad, decay in zip(masters, moms, varis, totals, decays)]
    fresh = tuple((item[0] for item in updated))
    fresh_moms = tuple((item[1] for item in updated))
    fresh_vars = tuple((item[2] for item in updated))
    return (block_out, grad_input, totals[0], totals[1], totals[2], totals[3], totals[4], totals[5], totals[6], fresh[0], fresh[1], fresh[2], fresh[3], fresh[4], fresh[5], fresh[6], fresh_moms[0], fresh_moms[1], fresh_moms[2], fresh_moms[3], fresh_moms[4], fresh_moms[5], fresh_moms[6], fresh_vars[0], fresh_vars[1], fresh_vars[2], fresh_vars[3], fresh_vars[4], fresh_vars[5], fresh_vars[6])
```

```python
import jax
import jax.numpy as jnp
from jax import lax
from jax.sharding import Mesh, PartitionSpec as P

HD = 256
SEQ = 2048
ADAM_STEP = 4


EPS = 1e-06
THETA = 1000000.0
LEARN = 0.02
BETA_ONE = 0.9
BETA_TWO = 0.95
ADAM_EPS = 1e-08
DECAY = 0.1
GELU_COEF = 0.7978845608028654
GELU_CUBE = 0.044715
NEG_FILL = -1e30

bf = jnp.bfloat16
fl = jnp.float32
DP = ("z", "y")


def rms_scale(values):
    return lax.rsqrt(jnp.mean(values * values, axis=-1, keepdims=True) + EPS)


def norm_back(values, scale, factor, incoming):
    scaled = incoming * factor
    return scale * (
        scaled - values * (scale * scale) * jnp.mean(scaled * values, axis=-1, keepdims=True)
    )


def rotate_half(values):
    middle = values.shape[-1] // 2
    return jnp.concatenate([-values[..., middle:], values[..., :middle]], axis=-1)


def rope_tables(position, width):
    middle = width // 2
    freqs = THETA ** (-2.0 * jnp.arange(middle, dtype=jnp.float32) / width)
    angle = position.astype(jnp.float32)[:, None] * freqs[None, :]
    cosine = jnp.concatenate([jnp.cos(angle), jnp.cos(angle)], axis=-1)
    sine = jnp.concatenate([jnp.sin(angle), jnp.sin(angle)], axis=-1)
    return (cosine, sine)


def gelu_parts(values):
    inner = GELU_COEF * (values + GELU_CUBE * values * values * values)
    tanh_val = jnp.tanh(inner)
    value = 0.5 * values * (1.0 + tanh_val)
    slope = 0.5 * (1.0 + tanh_val) + 0.5 * values * (1.0 - tanh_val * tanh_val) * GELU_COEF * (
        1.0 + 3.0 * GELU_CUBE * values * values
    )
    return (value, slope)


def adam_update(weight, mom, var, grad, decay):
    mom_new = BETA_ONE * mom + (1.0 - BETA_ONE) * grad
    var_new = BETA_TWO * var + (1.0 - BETA_TWO) * grad * grad
    fix_one = 1.0 - BETA_ONE**ADAM_STEP
    fix_two = 1.0 - BETA_TWO**ADAM_STEP
    direction = mom_new / fix_one / (jnp.sqrt(var_new / fix_two) + ADAM_EPS)
    return (weight - LEARN * (direction + decay * weight), mom_new, var_new)


def rotated(value, axis, by):
    size = lax.axis_size(axis)
    return lax.ppermute(value, axis, [(i, (i + by) % size) for i in range(size)])


def shifted(value, by):
    size = lax.axis_size(DP)
    return lax.ppermute(
        value, DP, [(i, i + by) for i in range(size) if 0 <= i + by < size]
    )


def pick(value, index):
    return lax.dynamic_index_in_dim(value, index, 0, keepdims=False)


def gather_axis(value, axis):
    size = lax.axis_size(axis)
    me = lax.axis_index(axis)
    if size == 2:
        other = rotated(value, axis, 1)
        return jnp.stack([jnp.where(me == 0, value, other), jnp.where(me == 0, other, value)])
    whole = jnp.zeros((size,) + value.shape, value.dtype)
    whole = lax.dynamic_update_index_in_dim(whole, value, me, 0)
    for by in range(1, size):
        whole = lax.dynamic_update_index_in_dim(
            whole, rotated(value, axis, by), (me - by) % size, 0
        )
    return whole


def scatter_axis(pieces, axis):
    size = lax.axis_size(axis)
    me = lax.axis_index(axis)
    total = pick(pieces, me).astype(fl)
    for by in range(1, size):
        sent = pick(pieces, (me + by) % size).astype(bf)
        total = total + rotated(sent, axis, by).astype(fl)
    return total


def scatter_model(partial):
    xs, cs = lax.axis_size("x"), lax.axis_size("c")
    rows, width = partial.shape
    view = partial.reshape(xs, cs, rows // (xs * cs), width)
    half = scatter_axis(view.swapaxes(0, 1), "c")
    return scatter_axis(half, "x")


def gather_model(part):
    both = gather_axis(part, "x")
    four = gather_axis(both, "c")
    four = four.swapaxes(0, 1)
    return four.reshape((-1,) + part.shape[1:])


def ring_order(size):
    return [0, 1, 3, 2] if size == 4 else list(range(size))


def ring_step(value):
    order = ring_order(lax.axis_size("z"))
    size = len(order)
    return lax.ppermute(value, "z", [(order[i], order[(i + 1) % size]) for i in range(size)])


def ring_place():
    order = ring_order(lax.axis_size("z"))
    place = [order.index(i) for i in range(len(order))]
    return jnp.array(order), pick(jnp.array(place), lax.axis_index("z"))


def gather_weights(block):
    order, place = ring_place()
    zs, ys = lax.axis_size("z"), lax.axis_size("y")
    kinds, rows, width = block.shape
    whole = jnp.zeros((kinds, zs * ys * rows, width), block.dtype)
    me = lax.axis_index("y")
    moving = block
    for step in range(zs):
        source = pick(order, (place - step) % zs)
        for by in range(ys):
            piece = moving if by == 0 else rotated(moving, "y", by)
            start = (source * ys + (me - by) % ys) * rows
            whole = lax.dynamic_update_slice_in_dim(whole, piece, start, 1)
        if step < zs - 1:
            moving = ring_step(moving)
    return whole


def scatter_weights(grads):
    order, place = ring_place()
    zs, ys = lax.axis_size("z"), lax.axis_size("y")
    kinds, total, width = grads.shape
    rows = total // (zs * ys)
    me = lax.axis_index("y")

    def summed(target):
        def piece(by):
            start = (target * ys + (me + by) % ys) * rows
            return lax.dynamic_slice_in_dim(grads, start, rows, 1).astype(bf)

        result = piece(0).astype(fl)
        for by in range(1, ys):
            result = result + rotated(piece(by), "y", by).astype(fl)
        return result

    running = summed(pick(order, (place - 1) % zs))
    for step in range(zs - 1):
        moved = ring_step(running.astype(bf))
        running = moved.astype(fl) + summed(pick(order, (place - step - 2) % zs))
    return running


def on_device(
    block_in,
    out_grad,
    segment_ids,
    w_query,
    w_keyval,
    w_out,
    w_gateup,
    w_down,
    gain_layers,
    gain_heads,
    mom_query,
    var_query,
    mom_keyval,
    var_keyval,
    mom_out,
    var_out,
    mom_gateup,
    var_gateup,
    mom_down,
    var_down,
    mom_layers,
    var_layers,
    mom_heads,
    var_heads,
):
    zs, ys = lax.axis_size("z"), lax.axis_size("y")
    xs, cs = lax.axis_size("x"), lax.axis_size("c")
    dps, mps = zs * ys, xs * cs
    model = lax.axis_index("x") * cs + lax.axis_index("c")
    device = lax.axis_index("z") * ys + lax.axis_index("y")
    width = HD
    rows, depth = block_in.shape
    quarter = rows // mps
    factor = width ** (-0.5)
    norm_factor = float(rows * dps) ** (-0.5)
    drows = w_query.shape[0]
    krows = w_keyval.shape[0]
    gcols, hcols = gain_layers.shape[1], gain_heads.shape[1]

    small = jnp.concatenate([gain_layers.reshape(-1), gain_heads.reshape(-1)]).astype(bf)
    small = jnp.pad(small, (0, width - small.shape[0])).reshape(1, width)
    keyval_halves = jnp.concatenate([w_keyval[:, :width], w_keyval[:, width:]], axis=0).astype(bf)
    pack = jnp.concatenate(
        [w_query.astype(bf), w_out.T.astype(bf), keyval_halves, small], axis=0
    )
    by_z = gather_axis(pack, "z")
    by_dp = gather_axis(by_z, "y").swapaxes(0, 1).reshape((dps,) + pack.shape)
    low_query = by_dp[:, :drows].reshape(depth, width)
    low_out = by_dp[:, drows : 2 * drows].reshape(depth, width)
    kv_mine = by_dp[:, 2 * drows :]
    kv_all = gather_axis(gather_axis(kv_mine, "x"), "c").swapaxes(0, 1)
    kv_all = kv_all.reshape((mps,) + kv_mine.shape).swapaxes(0, 1)
    low_key = kv_all[:, :, :krows].reshape(depth, width)
    low_value = kv_all[:, :, krows : 2 * krows].reshape(depth, width)
    gains = kv_all[:, :, 2 * krows].astype(fl)
    gain_scale = 1.0 + gains[:, :, : 4 * gcols].reshape(dps, mps, 4, gcols).transpose(
        2, 0, 1, 3
    ).reshape(4, depth)
    head_scale = 1.0 + gains[:, :, 4 * gcols : 4 * gcols + 2 * hcols].reshape(
        dps, mps, 2, hcols
    ).transpose(2, 0, 1, 3).reshape(2, width)
    low_keyval = jnp.concatenate([low_key, low_value], axis=1)

    low_ffn = gather_weights(
        jnp.concatenate([w_gateup.astype(bf), w_down.T.astype(bf)[None]], axis=0)
    )

    margin = SEQ // 2
    first_row = device * rows
    shifted_first = first_row + margin
    seq_start = shifted_first // SEQ * SEQ
    span = SEQ // rows
    position = shifted_first + jnp.arange(rows, dtype=jnp.int32)
    cosine, sine = rope_tables(position % SEQ, width)

    def part_rows(values):
        return lax.dynamic_slice_in_dim(values, model * quarter, quarter, 0)

    scale_in = rms_scale(block_in)
    normed_in = (block_in * scale_in * gain_scale[0]).astype(bf)
    keyval_raw = jnp.dot(normed_in, low_keyval, preferred_element_type=fl)
    key_raw = keyval_raw[:, :width]
    scale_key = rms_scale(key_raw)
    key_norm = key_raw * scale_key * head_scale[1]
    key_rot = key_norm * cosine + rotate_half(key_norm) * sine
    keyval_low = jnp.concatenate([key_rot, keyval_raw[:, width:]], axis=1).astype(bf)
    sent_kv = part_rows(keyval_low)
    earlier = jnp.stack([shifted(sent_kv, by) for by in range(span - 1, 0, -1)])
    four = gather_axis(gather_axis(earlier, "x"), "c")
    earlier = four.transpose(2, 1, 0, 3, 4).reshape((span - 1) * rows, 2 * width)
    window = jnp.concatenate([earlier, keyval_low], axis=0)
    seq_keys, seq_values = window[:, :width], window[:, width:]

    query_raw = jnp.dot(normed_in, low_query, preferred_element_type=fl)
    scale_query = rms_scale(query_raw)
    query_norm = query_raw * scale_query * head_scale[0]
    query_rot = (query_norm * cosine + rotate_half(query_norm) * sine).astype(bf)

    padded_seg = jnp.pad(segment_ids, (SEQ, 0), constant_values=-1)
    seg_query = lax.dynamic_slice_in_dim(segment_ids, first_row, rows, 0)
    reach = span * rows
    seg_keys = lax.dynamic_slice_in_dim(padded_seg, first_row + rows + SEQ - reach, reach, 0)
    key_index = shifted_first + rows - reach + jnp.arange(reach, dtype=jnp.int32)
    allowed = (
        (key_index[None, :] <= position[:, None])
        & (key_index[None, :] >= seq_start)
        & (seg_keys[None, :] == seg_query[:, None])
    )
    scores = jnp.einsum("qd,kd->qk", query_rot, seq_keys, preferred_element_type=fl) * factor
    masked = jnp.where(allowed, scores, NEG_FILL)
    top = jnp.max(masked, axis=-1, keepdims=True)
    log_total = top + jnp.log(jnp.sum(jnp.exp(masked - top), axis=-1, keepdims=True))
    probs = jnp.exp(masked - log_total)
    probs_low = probs.astype(bf)
    attended = jnp.dot(probs_low, seq_values, preferred_element_type=fl).astype(bf)

    in_part, scale_in_part = part_rows(block_in), part_rows(scale_in)
    grad_part = part_rows(out_grad)
    attn_proj = scatter_model(
        jnp.einsum("tc,dc->td", attended, low_out, preferred_element_type=fl)
    )
    scale_attn = rms_scale(attn_proj)
    resid = in_part + attn_proj * scale_attn * gain_scale[1]
    scale_mid = rms_scale(resid)
    normed_mid = gather_model((resid * scale_mid * gain_scale[2]).astype(bf))
    gate_raw = jnp.dot(normed_mid, low_ffn[0], preferred_element_type=fl)
    up_raw = jnp.dot(normed_mid, low_ffn[1], preferred_element_type=fl)
    gelu_value, gelu_slope = gelu_parts(gate_raw)
    hidden = (gelu_value * up_raw).astype(bf)
    ffn_proj = scatter_model(
        jnp.einsum("tf,df->td", hidden, low_ffn[2], preferred_element_type=fl)
    )
    scale_ffn = rms_scale(ffn_proj)
    out_part = resid + ffn_proj * scale_ffn * gain_scale[3]
    grad_ffn = gather_model(norm_back(ffn_proj, scale_ffn, gain_scale[3], grad_part).astype(bf))
    block_out = gather_model(out_part.astype(bf)).astype(fl)
    grad_down = jnp.einsum("td,tf->df", grad_ffn, hidden, preferred_element_type=fl).astype(bf)
    sum_down = scatter_weights(grad_down[None])[0].T
    grad_hidden = jnp.dot(grad_ffn, low_ffn[2], preferred_element_type=fl)
    grad_gate = (grad_hidden * up_raw * gelu_slope).astype(bf)
    grad_up = (grad_hidden * gelu_value).astype(bf)
    grad_mid = scatter_model(
        jnp.einsum("tf,df->td", grad_gate, low_ffn[0], preferred_element_type=fl)
        + jnp.einsum("tf,df->td", grad_up, low_ffn[1], preferred_element_type=fl)
    )
    grad_gateup = jnp.stack(
        [
            jnp.einsum("td,tf->df", normed_mid, grad_gate, preferred_element_type=fl).astype(bf),
            jnp.einsum("td,tf->df", normed_mid, grad_up, preferred_element_type=fl).astype(bf),
        ]
    )
    sum_gateup = scatter_weights(grad_gateup)
    grad_resid = grad_part + norm_back(resid, scale_mid, gain_scale[2], grad_mid)
    grad_attn = gather_model(
        norm_back(attn_proj, scale_attn, gain_scale[1], grad_resid).astype(bf)
    )
    grad_out = jnp.einsum("td,tc->dc", grad_attn, attended, preferred_element_type=fl)
    grad_attended = jnp.dot(grad_attn, low_out, preferred_element_type=fl).astype(bf)
    row_delta = jnp.sum(grad_attended.astype(fl) * attended.astype(fl), axis=-1, keepdims=True)
    grad_probs = jnp.einsum("qd,kd->qk", grad_attended, seq_values, preferred_element_type=fl)
    grad_scores = (probs * (grad_probs - row_delta) * factor).astype(bf)
    grad_qrot = jnp.dot(grad_scores, seq_keys, preferred_element_type=fl)
    grad_krot_seq = jnp.einsum("qk,qd->kd", grad_scores, query_rot, preferred_element_type=fl)
    grad_values_seq = jnp.einsum("qk,qd->kd", probs_low, grad_attended, preferred_element_type=fl)
    grad_seq = jnp.concatenate([grad_krot_seq, grad_values_seq], axis=1)
    by_model = grad_seq.reshape(span, xs, cs, quarter, 2 * width).transpose(2, 1, 0, 3, 4)
    by_block = scatter_axis(scatter_axis(by_model, "c"), "x")
    grad_kpart = by_block[span - 1]
    for by in range(1, span):
        grad_kpart = grad_kpart + shifted(by_block[span - 1 - by].astype(bf), -by).astype(fl)

    cos_part, sin_part = part_rows(cosine), part_rows(sine)
    key_part, scale_kpart = part_rows(key_raw), part_rows(scale_key)
    grad_krot = grad_kpart[:, :width]
    key_back = grad_krot * cos_part - rotate_half(grad_krot * sin_part)
    grad_kin = norm_back(key_part, scale_kpart, head_scale[1], key_back)
    grad_kvin = jnp.concatenate([grad_kin, grad_kpart[:, width:]], axis=1).astype(bf)
    keyval_part = jnp.einsum("tc,dc->td", grad_kvin, low_keyval, preferred_element_type=fl)
    grad_keyval = jnp.einsum(
        "td,tc->dc", normed_in, gather_model(grad_kvin), preferred_element_type=fl
    )
    grad_keyval = pick(grad_keyval.reshape(dps, mps, krows, 2 * width).swapaxes(0, 1), model)

    query_back = grad_qrot * cosine - rotate_half(grad_qrot * sine)
    grad_qin = norm_back(query_raw, scale_query, head_scale[0], query_back).astype(bf)
    grad_query = jnp.einsum("td,tc->dc", normed_in, grad_qin, preferred_element_type=fl)
    grad_normed = scatter_model(
        jnp.einsum("tc,dc->td", grad_qin, low_query, preferred_element_type=fl)
    ) + keyval_part
    grad_in_part = grad_resid + norm_back(in_part, scale_in_part, gain_scale[0], grad_normed)
    grad_input = gather_model(grad_in_part.astype(bf)).astype(fl)

    grad_layers = jnp.stack(
        [
            jnp.sum(grad_normed * in_part * scale_in_part, axis=0),
            jnp.sum(grad_resid * attn_proj * scale_attn, axis=0),
            jnp.sum(grad_mid * resid * scale_mid, axis=0),
            jnp.sum(grad_part * ffn_proj * scale_ffn, axis=0),
        ]
    )
    grad_heads = jnp.stack(
        [
            jnp.sum(query_back * query_raw * scale_query, axis=0),
            jnp.sum(key_back * key_part * scale_kpart, axis=0),
        ]
    )
    grad_small = jnp.concatenate(
        [
            grad_layers.reshape(4, dps, mps, gcols).transpose(1, 2, 0, 3).reshape(dps, mps, -1),
            grad_heads.reshape(2, dps, mps, hcols).transpose(1, 2, 0, 3).reshape(dps, mps, -1),
        ],
        axis=2,
    )
    grad_small = jnp.pad(grad_small, ((0, 0), (0, 0), (0, width - grad_small.shape[2])))
    grad_small = grad_small.reshape(dps, xs, cs, width).transpose(2, 1, 0, 3)
    grad_small = scatter_axis(scatter_axis(grad_small, "c"), "x")
    grad_pack = jnp.concatenate(
        [
            grad_query.reshape(dps, drows, width).astype(bf),
            grad_out.reshape(dps, drows, width).astype(bf),
            grad_keyval[:, :, :width].astype(bf),
            grad_keyval[:, :, width:].astype(bf),
            grad_small[:, None].astype(bf),
        ],
        axis=1,
    )
    sums_pack = scatter_axis(
        scatter_axis(grad_pack.reshape((zs, ys) + grad_pack.shape[1:]).swapaxes(0, 1), "y"), "z"
    )
    sum_query = sums_pack[:drows]
    sum_out = sums_pack[drows : 2 * drows].T
    sum_keyval = jnp.concatenate(
        [
            sums_pack[2 * drows : 2 * drows + krows],
            sums_pack[2 * drows + krows : 2 * drows + 2 * krows],
        ],
        axis=1,
    )
    sum_small = sums_pack[2 * drows + 2 * krows]
    sum_layers = sum_small[: 4 * gcols].reshape(4, gcols)
    sum_heads = sum_small[4 * gcols : 4 * gcols + 2 * hcols].reshape(2, hcols)

    masters = (w_query, w_keyval, w_out, w_gateup, w_down, gain_layers, gain_heads)
    sums = (sum_query, sum_keyval, sum_out, sum_gateup, sum_down, sum_layers, sum_heads)
    totals = tuple((item * norm_factor for item in sums))
    moms = (mom_query, mom_keyval, mom_out, mom_gateup, mom_down, mom_layers, mom_heads)
    varis = (var_query, var_keyval, var_out, var_gateup, var_down, var_layers, var_heads)
    decays = (DECAY, DECAY, DECAY, DECAY, DECAY, 0.0, 0.0)
    updated = [
        adam_update(master, mom, var, grad, decay)
        for master, mom, var, grad, decay in zip(masters, moms, varis, totals, decays)
    ]
    return (
        (block_out, grad_input)
        + totals
        + tuple(item[0] for item in updated)
        + tuple(item[1] for item in updated)
        + tuple(item[2] for item in updated)
    )


def solution(mesh):
    dps, mps = mesh.shape["dp"], mesh.shape["mp"]
    zs = 4 if dps % 4 == 0 else 1
    cs = 2 if mps % 2 == 0 else 1
    split = Mesh(mesh.devices.reshape(zs, dps // zs, mps // cs, cs), ("z", "y", "x", "c"))
    mp = ("x", "c")
    both = DP + mp
    weights = (
        P(DP, mp),
        P(both, None),
        P(mp, DP),
        P(None, DP, mp),
        P(mp, DP),
        P(None, both),
        P(None, both),
    )
    tokens = P(DP, None)
    states = tuple(spec for spec in weights for _ in range(2))
    in_specs = (tokens, tokens, P()) + weights + states
    out_specs = (tokens, tokens) + weights * 4
    return jax.shard_map(
        on_device, mesh=split, in_specs=in_specs, out_specs=out_specs, check_vma=False
    )
```

```python
import functools

import jax
import jax.numpy as jnp
import numpy as np
from jax import lax
from jax.experimental import pallas as pl
from jax.experimental.pallas import tpu as pltpu
from jax.sharding import Mesh, PartitionSpec as P

HD = 256
SEQ = 2048
ADAM_STEP = 4


EPS = 1e-06
THETA = 1000000.0
LEARN = 0.02
BETA_ONE = 0.9
BETA_TWO = 0.95
ADAM_EPS = 1e-08
DECAY = 0.1
GELU_COEF = 0.7978845608028654
GELU_CUBE = 0.044715
NEG_FILL = -1e30

bf = jnp.bfloat16
fl = jnp.float32
DP = ("z", "y")


def rms_scale(values):
    return lax.rsqrt(jnp.mean(values * values, axis=-1, keepdims=True) + EPS)


def norm_back(values, scale, factor, incoming):
    scaled = incoming * factor
    return scale * (
        scaled - values * (scale * scale) * jnp.mean(scaled * values, axis=-1, keepdims=True)
    )


def rotate_half(values):
    middle = values.shape[-1] // 2
    return jnp.concatenate([-values[..., middle:], values[..., :middle]], axis=-1)


def rope_tables(position, width):
    middle = width // 2
    freqs = THETA ** (-2.0 * jnp.arange(middle, dtype=jnp.float32) / width)
    angle = position.astype(jnp.float32)[:, None] * freqs[None, :]
    cosine = jnp.concatenate([jnp.cos(angle), jnp.cos(angle)], axis=-1)
    sine = jnp.concatenate([jnp.sin(angle), jnp.sin(angle)], axis=-1)
    return (cosine, sine)


def gelu_parts(values):
    inner = GELU_COEF * (values + GELU_CUBE * values * values * values)
    tanh_val = jnp.tanh(inner)
    value = 0.5 * values * (1.0 + tanh_val)
    slope = 0.5 * (1.0 + tanh_val) + 0.5 * values * (1.0 - tanh_val * tanh_val) * GELU_COEF * (
        1.0 + 3.0 * GELU_CUBE * values * values
    )
    return (value, slope)


def adam_update(weight, mom, var, grad, decay):
    mom_new = BETA_ONE * mom + (1.0 - BETA_ONE) * grad
    var_new = BETA_TWO * var + (1.0 - BETA_TWO) * grad * grad
    fix_one = 1.0 - BETA_ONE**ADAM_STEP
    fix_two = 1.0 - BETA_TWO**ADAM_STEP
    direction = mom_new / fix_one / (jnp.sqrt(var_new / fix_two) + ADAM_EPS)
    return (weight - LEARN * (direction + decay * weight), mom_new, var_new)


def rotated(value, axis, by):
    size = lax.axis_size(axis)
    return lax.ppermute(value, axis, [(i, (i + by) % size) for i in range(size)])


def shifted(value, by):
    size = lax.axis_size(DP)
    return lax.ppermute(
        value, DP, [(i, i + by) for i in range(size) if 0 <= i + by < size]
    )


def pick(value, index):
    return lax.dynamic_index_in_dim(value, index, 0, keepdims=False)


def gather_axis(value, axis):
    size = lax.axis_size(axis)
    me = lax.axis_index(axis)
    if size == 2:
        other = rotated(value, axis, 1)
        return jnp.stack([jnp.where(me == 0, value, other), jnp.where(me == 0, other, value)])
    whole = jnp.zeros((size,) + value.shape, value.dtype)
    whole = lax.dynamic_update_index_in_dim(whole, value, me, 0)
    for by in range(1, size):
        whole = lax.dynamic_update_index_in_dim(
            whole, rotated(value, axis, by), (me - by) % size, 0
        )
    return whole


def scatter_axis(pieces, axis):
    size = lax.axis_size(axis)
    me = lax.axis_index(axis)
    total = pick(pieces, me).astype(fl)
    for by in range(1, size):
        sent = pick(pieces, (me + by) % size).astype(bf)
        total = total + rotated(sent, axis, by).astype(fl)
    return total


def scatter_model(partial):
    xs, cs = lax.axis_size("x"), lax.axis_size("c")
    rows, width = partial.shape
    view = partial.reshape(xs, cs, rows // (xs * cs), width)
    half = scatter_axis(view.swapaxes(0, 1), "c")
    return scatter_axis(half, "x")


def gather_model(part):
    both = gather_axis(part, "x")
    four = gather_axis(both, "c")
    four = four.swapaxes(0, 1)
    return four.reshape((-1,) + part.shape[1:])


def ring_index(index, size):
    return index ^ (index >> 1) if size == 4 else index


def ring_step(value):
    size = lax.axis_size("z")
    pairs = [(ring_index(i, size), ring_index((i + 1) % size, size)) for i in range(size)]
    return lax.ppermute(value, "z", pairs)


def ring_source(back):
    size = lax.axis_size("z")
    place = ring_index(lax.axis_index("z"), size)
    return ring_index((place - back + size) % size, size)


def after(value, *others):
    return lax.optimization_barrier((value,) + others)[0]


def over_y(value):
    return [rotated(value, "y", by) for by in range(1, lax.axis_size("y"))]


def in_order(blocks):
    zs, ys = lax.axis_size("z"), lax.axis_size("y")
    me = lax.axis_index("y")
    whole = jnp.zeros((zs * ys,) + blocks[0][0].shape, blocks[0][0].dtype)
    for step, row in enumerate(blocks):
        source = ring_source(step)
        for by, piece in enumerate(row):
            whole = lax.dynamic_update_index_in_dim(
                whole, piece, source * ys + (me - by) % ys, 0
            )
    return whole


TILE = 256
NOMINAL = pl.CostEstimate(flops=1, bytes_accessed=1, transcendentals=0)


def _columns(block, index, valid):
    at = index * TILE + lax.broadcasted_iota(jnp.int32, block.shape, 1)
    return jnp.where(at < valid, block, jnp.zeros_like(block))


def _flat(block):
    return block.reshape(-1, block.shape[-1])


def _hidden_kernel(valid, mid_ref, w_ref, hid_ref, gate_ref, up_ref):
    mid = mid_ref[...]
    gate = jnp.dot(mid, _flat(w_ref[:, 0]), preferred_element_type=fl)
    up = jnp.dot(mid, _flat(w_ref[:, 1]), preferred_element_type=fl)
    value, slope = gelu_parts(gate)
    hid_ref[...] = (value * up).astype(bf)
    gate_ref[...] = (up * slope).astype(bf)
    up_ref[...] = value.astype(bf)


def _down_kernel(valid, hid_ref, down_ref, out_ref):
    index = pl.program_id(0)

    def add(hid, down):
        part = lax.dot_general(hid, down, (((1,), (1,)), ((), ())), preferred_element_type=fl)

        @pl.when(index == 0)
        def _():
            out_ref[...] = part

        @pl.when(index > 0)
        def _():
            out_ref[...] += part

    last = index == pl.num_programs(0) - 1

    @pl.when(jnp.logical_not(last))
    def _():
        add(hid_ref[...], _flat(down_ref[:, 0]))

    @pl.when(last)
    def _():
        add(_columns(hid_ref[...], index, valid), _columns(_flat(down_ref[:, 0]), index, valid))


def _backward_kernel(valid, ffn_ref, gate_ref, up_ref, w_ref, down_ref, mid_ref, ggate_ref, gup_ref):
    index = pl.program_id(0)
    grad = jnp.dot(ffn_ref[...], _flat(down_ref[:, 0]), preferred_element_type=fl)
    ggate = (grad * gate_ref[...].astype(fl)).astype(bf)
    gup = (grad * up_ref[...].astype(fl)).astype(bf)
    ggate_ref[...] = ggate
    gup_ref[...] = gup

    def add(one, two, w_one, w_two):
        dims = (((1,), (1,)), ((), ()))
        part = lax.dot_general(one, w_one, dims, preferred_element_type=fl)
        part = part + lax.dot_general(two, w_two, dims, preferred_element_type=fl)

        @pl.when(index == 0)
        def _():
            mid_ref[...] = part

        @pl.when(index > 0)
        def _():
            mid_ref[...] += part

    last = index == pl.num_programs(0) - 1
    w_one, w_two = _flat(w_ref[:, 0]), _flat(w_ref[:, 1])

    @pl.when(jnp.logical_not(last))
    def _():
        add(ggate, gup, w_one, w_two)

    @pl.when(last)
    def _():
        add(
            _columns(ggate, index, valid),
            _columns(gup, index, valid),
            _columns(w_one, index, valid),
            _columns(w_two, index, valid),
        )


def _grads_kernel(pairs, left_ref, *refs):
    turned = refs[-1]

    @pl.when(pl.program_id(0) == 0)
    def _():
        turned[...] = left_ref[...].T

    for right_ref, out_ref in zip(refs[:pairs], refs[pairs : 2 * pairs]):
        grads = jnp.dot(turned[...], right_ref[...], preferred_element_type=fl).astype(bf)
        out_ref[...] = grads.reshape(out_ref.shape)


def grads_call(left, rights, pieces, name):
    rows, depth = left.shape
    units = rights[0].shape[1]
    split = pieces if depth // pieces % 16 == 0 else 1
    shape = (split, depth // split, units)
    column = pl.BlockSpec((rows, TILE), lambda j: (0, j))
    out = pl.BlockSpec(shape[:2] + (TILE,), lambda j: (0, 0, j))
    results = pl.pallas_call(
        functools.partial(_grads_kernel, len(rights)),
        out_shape=[jax.ShapeDtypeStruct(shape, bf)] * len(rights),
        grid=(pl.cdiv(units, TILE),),
        in_specs=[pl.BlockSpec((rows, depth), lambda j: (0, 0))] + [column] * len(rights),
        out_specs=[out] * len(rights),
        scratch_shapes=[pltpu.VMEM((depth, rows), bf)],
        compiler_params=pltpu.CompilerParams(
            dimension_semantics=("arbitrary",), vmem_limit_bytes=40 * 1024 * 1024
        ),
        cost_estimate=NOMINAL,
        name=name,
    )(left, *rights)
    return [result.reshape(pieces, depth // pieces, units) for result in results]


def ffn_call(kernel, name, rows, lefts, weights, tiles_in, total, tiles_out):
    units = weights[0].shape[-1]
    depth = weights[0].shape[0] * weights[0].shape[2]
    kinds = sum(w.shape[1] for w in weights)
    column = pl.BlockSpec((rows, TILE), lambda j: (0, j))
    whole = pl.BlockSpec((rows, depth), lambda j: (0, 0))
    tile = jax.ShapeDtypeStruct((rows, units), bf)
    return pl.pallas_call(
        functools.partial(kernel, units),
        out_shape=[jax.ShapeDtypeStruct((rows, depth), fl)] * total + [tile] * tiles_out,
        grid=(pl.cdiv(units, TILE),),
        in_specs=[whole] * len(lefts)
        + [column] * len(tiles_in)
        + [pl.BlockSpec(w.shape[:3] + (TILE,), lambda j: (0, 0, 0, j)) for w in weights],
        out_specs=[whole] * total + [column] * tiles_out,
        compiler_params=pltpu.CompilerParams(
            dimension_semantics=("arbitrary",), vmem_limit_bytes=40 * 1024 * 1024
        ),
        cost_estimate=NOMINAL,
        name=name,
    )(*lefts, *tiles_in, *weights)


HALVES = 2


def row_call(kernel, name, rows, by_rows, whole, out_rows, out_whole=(), scratch=()):
    step = rows // HALVES

    def cut(shape):
        return pl.BlockSpec((step,) + shape[1:], lambda i: (i, 0))

    def kept(shape):
        return pl.BlockSpec(shape, lambda i: (0,) * len(shape))

    return pl.pallas_call(
        kernel,
        out_shape=[jax.ShapeDtypeStruct(*item) for item in list(out_rows) + list(out_whole)],
        grid=(HALVES,),
        in_specs=[cut(item.shape) for item in by_rows] + [kept(item.shape) for item in whole],
        out_specs=[cut(item[0]) for item in out_rows] + [kept(item[0]) for item in out_whole],
        scratch_shapes=scratch,
        compiler_params=pltpu.CompilerParams(
            dimension_semantics=("arbitrary",), vmem_limit_bytes=48 * 1024 * 1024
        ),
        cost_estimate=NOMINAL,
        name=name,
    )(*by_rows, *whole)


def _project_kernel(
    x_ref,
    cos_ref,
    sin_ref,
    gain_ref,
    head_ref,
    query_ref,
    keyval_ref,
    normed_ref,
    scale_ref,
    qraw_ref,
    qscale_ref,
    qrot_ref,
    kraw_ref,
    kscale_ref,
    kv_ref,
):
    width = qraw_ref.shape[1]
    values = x_ref[...]
    scale = rms_scale(values)
    scale_ref[...] = scale
    normed = (values * scale * gain_ref[...]).astype(bf)
    normed_ref[...] = normed
    cosine, sine = cos_ref[...], sin_ref[...]

    def turned(raw, scale, factor):
        norm = raw * scale * factor
        return (norm * cosine + rotate_half(norm) * sine).astype(bf)

    raw = jnp.dot(normed, query_ref[...], preferred_element_type=fl)
    scale = rms_scale(raw)
    qraw_ref[...] = raw
    qscale_ref[...] = scale
    qrot_ref[...] = turned(raw, scale, head_ref[0:1])
    raw = jnp.dot(normed, keyval_ref[...], preferred_element_type=fl)
    key = raw[:, :width]
    scale = rms_scale(key)
    kraw_ref[...] = key
    kscale_ref[...] = scale
    kv_ref[:, :width] = turned(key, scale, head_ref[1:2])
    kv_ref[:, width:] = raw[:, width:].astype(bf)


ACROSS = (((1,), (1,)), ((), ()))


def _masked_scores(query, keys, low, high, factor):
    scores = lax.dot_general(query, keys, ACROSS, preferred_element_type=fl) * factor
    at = lax.broadcasted_iota(jnp.int32, scores.shape, 1)
    return jnp.where((at >= low) & (at <= high), scores, NEG_FILL)


def _attend_kernel(
    factor, query_ref, low_ref, high_ref, window_ref, out_ref, att_ref, log_ref, part_ref
):
    width = query_ref.shape[1]
    masked = _masked_scores(
        query_ref[...], window_ref[:, :width], low_ref[...], high_ref[...], factor
    )
    top = jnp.max(masked, axis=-1, keepdims=True)
    powers = jnp.exp(masked - top)
    total = jnp.sum(powers, axis=-1, keepdims=True)
    log_ref[...] = top + jnp.log(total)
    probs = (powers * (1.0 / total)).astype(bf)
    attended = jnp.dot(probs, window_ref[:, width:], preferred_element_type=fl).astype(bf)
    att_ref[...] = attended
    part_ref[...] = lax.dot_general(attended, out_ref[...], ACROSS, preferred_element_type=fl)


def _attend_back_kernel(
    factor,
    grad_ref,
    query_ref,
    low_ref,
    high_ref,
    log_ref,
    att_ref,
    qraw_ref,
    qscale_ref,
    cos_ref,
    sin_ref,
    head_ref,
    window_ref,
    out_ref,
    lowq_ref,
    gqin_ref,
    part_ref,
    gkv_ref,
    ghead_ref,
    turned,
):
    width = query_ref.shape[1]
    keys, values = window_ref[:, :width], window_ref[:, width:]
    query = query_ref[...]
    grad_att = jnp.dot(grad_ref[...], out_ref[...], preferred_element_type=fl).astype(bf)
    delta = jnp.sum(
        grad_att.astype(fl) * att_ref[...].astype(fl), axis=-1, keepdims=True
    )
    masked = _masked_scores(query, keys, low_ref[...], high_ref[...], factor)
    probs = jnp.exp(masked - log_ref[...])
    grad_probs = lax.dot_general(grad_att, values, ACROSS, preferred_element_type=fl)
    grad_scores = (probs * (grad_probs - delta) * factor).astype(bf)
    grad_q = jnp.dot(grad_scores, keys, preferred_element_type=fl)
    grad_k = jnp.dot(query.T, grad_scores, preferred_element_type=fl)
    grad_v = jnp.dot(grad_att.T, probs.astype(bf), preferred_element_type=fl)
    back = grad_q * cos_ref[...] - rotate_half(grad_q * sin_ref[...])
    raw, scale = qraw_ref[...], qscale_ref[...]
    gqin = norm_back(raw, scale, head_ref[0:1], back).astype(bf)
    gqin_ref[...] = gqin
    part_ref[...] = lax.dot_general(gqin, lowq_ref[...], ACROSS, preferred_element_type=fl)
    ghead = jnp.sum(back * raw * scale, axis=0, keepdims=True)
    first = pl.program_id(0) == 0

    @pl.when(first)
    def _():
        turned[:width] = grad_k
        turned[width:] = grad_v
        ghead_ref[...] = ghead

    @pl.when(jnp.logical_not(first))
    def _():
        turned[:width] += grad_k
        turned[width:] += grad_v
        ghead_ref[...] += ghead

    @pl.when(pl.program_id(0) == pl.num_programs(0) - 1)
    def _():
        gkv_ref[...] = turned[...].astype(bf).T


def on_device(
    block_in,
    out_grad,
    segment_ids,
    w_query,
    w_keyval,
    w_out,
    w_gateup,
    w_down,
    gain_layers,
    gain_heads,
    mom_query,
    var_query,
    mom_keyval,
    var_keyval,
    mom_out,
    var_out,
    mom_gateup,
    var_gateup,
    mom_down,
    var_down,
    mom_layers,
    var_layers,
    mom_heads,
    var_heads,
):
    zs, ys = lax.axis_size("z"), lax.axis_size("y")
    xs, cs = lax.axis_size("x"), lax.axis_size("c")
    dps, mps = zs * ys, xs * cs
    model = lax.axis_index("x") * cs + lax.axis_index("c")
    device = lax.axis_index("z") * ys + lax.axis_index("y")
    width = HD
    rows, depth = block_in.shape
    quarter = rows // mps
    factor = width ** (-0.5)
    norm_factor = float(rows * dps) ** (-0.5)
    drows = w_query.shape[0]
    krows = w_keyval.shape[0]
    gcols, hcols = gain_layers.shape[1], gain_heads.shape[1]

    kpad = -(-krows // 16) * 16
    small = jnp.concatenate([gain_layers.reshape(-1), gain_heads.reshape(-1)]).astype(bf)
    small = jnp.pad(small, (0, width - small.shape[0])).reshape(1, width)
    fill = jnp.zeros((kpad - krows, width), bf)
    pack = jnp.concatenate(
        [
            w_query.astype(bf),
            w_keyval[:, :width].astype(bf),
            fill,
            w_keyval[:, width:].astype(bf),
            fill,
            jnp.pad(small, ((0, 15), (0, 0))),
        ],
        axis=0,
    )
    by_z = gather_axis(pack, "z")
    by_dp = gather_axis(by_z, "y").swapaxes(0, 1).reshape((dps,) + pack.shape)
    low_query = by_dp[:, :drows].reshape(depth, width)
    kv_mine = by_dp[:, drows:]

    gateup0, down0 = w_gateup.astype(bf), w_down.T.astype(bf)
    gateup1 = ring_step(after(gateup0, by_z))
    gateup0_y = over_y(after(gateup0, by_dp))
    gateup2 = ring_step(gateup1)
    gateup1_y = over_y(after(gateup1, *gateup0_y))
    gateup3 = ring_step(gateup2)
    down_y = over_y(after(down0, *gateup1_y))

    kv_all = gather_axis(gather_axis(after(kv_mine, gateup1), "x"), "c")
    kv_all = after(kv_all, gateup2, *gateup0_y)
    lanes = np.arange(cs * xs * dps * kpad).reshape(cs, xs, dps, kpad)
    core, xx, dd, rr = np.unravel_index(lanes.reshape(-1), lanes.shape)
    owner = np.where(rr < krows, (dd * mps + xx * cs + core) * krows + rr, -1)
    depth_index = jnp.arange(depth, dtype=jnp.int32)
    sorter = (depth_index[:, None] == jnp.asarray(owner, jnp.int32)[None, :]).astype(bf)
    kv_pad = jnp.concatenate(
        [
            kv_all[:, :, :, :kpad].reshape(-1, width),
            kv_all[:, :, :, kpad : 2 * kpad].reshape(-1, width),
        ],
        axis=1,
    )
    low_keyval = jnp.dot(sorter, kv_pad, preferred_element_type=fl).astype(bf)
    low_keyval = after(low_keyval, gateup3, *gateup1_y)
    mine = np.arange(dps * kpad)
    owner = (mine // kpad) * mps * krows + mine % kpad
    owner = jnp.asarray(owner, jnp.int32) + model * krows
    chooser = (depth_index[:, None] == owner[None, :]) & jnp.asarray(mine % kpad < krows)[None, :]
    gains = kv_all[:, :, :, 2 * kpad].astype(fl)
    gain_scale = 1.0 + gains[:, :, :, : 4 * gcols].reshape(cs, xs, dps, 4, gcols).transpose(
        3, 2, 1, 0, 4
    ).reshape(4, depth)
    head_scale = 1.0 + gains[:, :, :, 4 * gcols : 4 * gcols + 2 * hcols].reshape(
        cs, xs, dps, 2, hcols
    ).transpose(3, 2, 1, 0, 4).reshape(2, width)

    margin = SEQ // 2
    first_row = device * rows
    shifted_first = first_row + margin
    seq_start = shifted_first // SEQ * SEQ
    span = SEQ // rows
    position = shifted_first + jnp.arange(rows, dtype=jnp.int32)
    cosine, sine = rope_tables(position % SEQ, width)

    def part_rows(values):
        return lax.dynamic_slice_in_dim(values, model * quarter, quarter, 0)

    (
        normed_in,
        scale_in,
        query_raw,
        scale_query,
        query_rot,
        key_raw,
        scale_key,
        keyval_low,
    ) = row_call(
        _project_kernel,
        "project",
        rows,
        [block_in, cosine, sine],
        [gain_scale[0:1], head_scale, low_query, low_keyval],
        [
            ((rows, depth), bf),
            ((rows, 1), fl),
            ((rows, width), fl),
            ((rows, 1), fl),
            ((rows, width), bf),
            ((rows, width), fl),
            ((rows, 1), fl),
            ((rows, 2 * width), bf),
        ],
    )
    sent_kv = after(part_rows(keyval_low), *down_y)
    earlier = jnp.stack([shifted(sent_kv, by) for by in range(span - 1, 0, -1)])
    out_by_z = gather_axis(after(w_out.T.astype(bf), sent_kv), "z")
    low_out = gather_axis(out_by_z, "y").swapaxes(0, 1).reshape(depth, width)
    down0 = after(jnp.stack([down0] + down_y), earlier, out_by_z)
    down1 = ring_step(down0)
    gateup2_y = over_y(after(gateup2, earlier, low_out))
    four = gather_axis(gather_axis(earlier, "x"), "c")
    earlier = four.transpose(2, 1, 0, 3, 4).reshape((span - 1) * rows, 2 * width)
    earlier = after(earlier, down1, *gateup2_y)
    window = jnp.concatenate([earlier, keyval_low], axis=0)
    reach = span * rows
    window_first = first_row + rows - reach
    seg_query = lax.dynamic_slice_in_dim(segment_ids, first_row, rows, 0)
    doc_first = jnp.sum(
        (segment_ids[None, :] < seg_query[:, None]).astype(jnp.int32), axis=1, keepdims=True
    )
    run_first = jnp.maximum(doc_first, seq_start - margin) - window_first
    run_last = jnp.arange(rows, dtype=jnp.int32)[:, None] + (reach - rows)
    attended, log_total, attn_part = row_call(
        functools.partial(_attend_kernel, factor),
        "attend",
        rows,
        [query_rot, run_first, run_last],
        [window, low_out],
        [((rows, width), bf), ((rows, 1), fl), ((rows, depth), fl)],
    )
    down2 = ring_step(down1)
    gateup3_y = over_y(after(gateup3, *gateup2_y))

    in_part, scale_in_part = part_rows(block_in), part_rows(scale_in)
    grad_part = part_rows(out_grad)
    attn_proj = after(scatter_model(attn_part), down2, *gateup3_y)
    down3 = ring_step(down2)
    scale_attn = rms_scale(attn_proj)
    resid = in_part + attn_proj * scale_attn * gain_scale[1]
    scale_mid = rms_scale(resid)
    normed_mid = gather_model((resid * scale_mid * gain_scale[2]).astype(bf))
    low_gateup = in_order(
        [
            [gateup0] + gateup0_y,
            [gateup1] + gateup1_y,
            [gateup2] + gateup2_y,
            [gateup3] + gateup3_y,
        ]
    )
    low_down = in_order([[block[by] for by in range(ys)] for block in (down0, down1, down2, down3)])
    low_down = low_down[:, None]
    if drows % 16:
        low_gateup = low_gateup.swapaxes(0, 1).reshape((1, 2, depth, -1))
        low_down = low_down.reshape((1, 1, depth, -1))
    hidden, gate_factor, up_factor = ffn_call(
        _hidden_kernel, "ffn_hidden", rows, [normed_mid], [low_gateup], [], 0, 3
    )
    (ffn_part,) = ffn_call(_down_kernel, "ffn_down", rows, [], [low_down], [hidden], 1, 0)
    ffn_proj = scatter_model(ffn_part)
    scale_ffn = rms_scale(ffn_proj)
    out_part = resid + ffn_proj * scale_ffn * gain_scale[3]
    grad_ffn = gather_model(norm_back(ffn_proj, scale_ffn, gain_scale[3], grad_part).astype(bf))
    (grad_down,) = grads_call(grad_ffn, [hidden], dps, "down_grads")
    grad_down = grad_down.reshape((zs, ys) + grad_down.shape[1:])
    sum_down1 = ring_step(pick(grad_down, ring_source(1)))
    grad_ffn = after(grad_ffn, grad_down)
    mid_part, grad_gate, grad_up = ffn_call(
        _backward_kernel,
        "ffn_backward",
        rows,
        [grad_ffn],
        [low_gateup, low_down],
        [gate_factor, up_factor],
        1,
        2,
    )
    grads_gateup = grads_call(normed_mid, [grad_gate, grad_up], dps, "gateup_grads")

    def gateup_piece(target, by):
        index = ring_source(target) * ys + (lax.axis_index("y") + by) % ys
        return jnp.stack([pick(item, index) for item in grads_gateup])

    def gateup_over_y(target, *others):
        total = gateup_piece(target, 0).astype(fl)
        for by in range(1, ys):
            sent = after(gateup_piece(target, by), *others)
            total = total + rotated(sent, "y", by).astype(fl)
        return total

    def down_add(came, target):
        return came.astype(fl) + pick(grad_down, ring_source(target)).astype(fl)

    gateup_a = gateup_over_y(1)
    gateup_b = gateup_over_y(2, gateup_a)
    gateup_c = gateup_over_y(3, gateup_b)
    gateup_d = gateup_over_y(4, gateup_c)
    sum_down2 = ring_step(down_add(sum_down1, 2).astype(bf))
    sum_down3 = ring_step(down_add(sum_down2, 3).astype(bf))
    grad_mid = after(scatter_model(after(mid_part, sum_down1)), sum_down2)
    block_out = gather_model(after(out_part, grad_mid).astype(bf)).astype(fl)
    grad_resid = grad_part + norm_back(resid, scale_mid, gain_scale[2], grad_mid)
    grad_attn = gather_model(
        norm_back(attn_proj, scale_attn, gain_scale[1], grad_resid).astype(bf)
    )
    grad_attn = after(grad_attn, sum_down3, gateup_a)
    sum_gateup1 = ring_step(after(gateup_a, sum_down3).astype(bf))
    sum_gateup2 = ring_step((sum_gateup1.astype(fl) + gateup_b).astype(bf))
    grad_out = jnp.einsum("td,tc->dc", grad_attn, attended, preferred_element_type=fl)
    grad_qin, normed_part, grad_seq, grad_qhead = row_call(
        functools.partial(_attend_back_kernel, factor),
        "attend_back",
        rows,
        [
            grad_attn,
            query_rot,
            run_first,
            run_last,
            log_total,
            attended,
            query_raw,
            scale_query,
            cosine,
            sine,
        ],
        [head_scale, window, low_out, low_query],
        [((rows, width), bf), ((rows, depth), fl)],
        [((reach, 2 * width), bf), ((1, width), fl)],
        [pltpu.VMEM((2 * width, reach), fl)],
    )
    by_model = grad_seq.reshape(span, xs, cs, quarter, 2 * width).transpose(2, 1, 0, 3, 4)
    by_block = after(scatter_axis(by_model, "c"), sum_gateup1, gateup_b)
    by_block = after(scatter_axis(by_block, "x"), sum_gateup2, gateup_d)
    grad_kpart = by_block[span - 1]
    for by in range(1, span):
        grad_kpart = grad_kpart + shifted(by_block[span - 1 - by].astype(bf), -by).astype(fl)

    sum_gateup3 = after(sum_gateup2.astype(fl) + gateup_c, grad_kpart)
    sum_gateup3 = ring_step(sum_gateup3.astype(bf))
    sum_down = down_add(sum_down3, 4)
    own = lax.axis_index("y")
    sum_down_own = pick(sum_down, own)
    for by in range(1, ys):
        sent = after(pick(sum_down, (own + by) % ys).astype(bf), gateup_d)
        sum_down_own = sum_down_own + rotated(sent, "y", by).astype(fl)
    sum_down = sum_down_own.T

    cos_part, sin_part = part_rows(cosine), part_rows(sine)
    key_part, scale_kpart = part_rows(key_raw), part_rows(scale_key)
    grad_krot = grad_kpart[:, :width]
    key_back = grad_krot * cos_part - rotate_half(grad_krot * sin_part)
    grad_kin = norm_back(key_part, scale_kpart, head_scale[1], key_back)
    grad_kvin = jnp.concatenate([grad_kin, grad_kpart[:, width:]], axis=1).astype(bf)
    keyval_part = jnp.einsum("tc,dc->td", grad_kvin, low_keyval, preferred_element_type=fl)
    normed_mine = jnp.dot(normed_in, chooser.astype(bf), preferred_element_type=fl).astype(bf)
    grad_keyval = jnp.einsum(
        "td,tc->dc", normed_mine, gather_model(grad_kvin), preferred_element_type=fl
    ).reshape(dps, kpad, 2 * width)

    grad_query = jnp.einsum("td,tc->dc", normed_in, grad_qin, preferred_element_type=fl)
    grad_normed = scatter_model(normed_part) + keyval_part
    grad_in_part = grad_resid + norm_back(in_part, scale_in_part, gain_scale[0], grad_normed)
    grad_input = gather_model(grad_in_part.astype(bf)).astype(fl)

    grad_layers = jnp.stack(
        [
            jnp.sum(grad_normed * in_part * scale_in_part, axis=0),
            jnp.sum(grad_resid * attn_proj * scale_attn, axis=0),
            jnp.sum(grad_mid * resid * scale_mid, axis=0),
            jnp.sum(grad_part * ffn_proj * scale_ffn, axis=0),
        ]
    )
    grad_heads = jnp.stack(
        [
            grad_qhead[0],
            jnp.sum(key_back * key_part * scale_kpart, axis=0),
        ]
    )
    grad_small = jnp.concatenate(
        [
            grad_layers.reshape(4, dps, mps, gcols).transpose(1, 2, 0, 3).reshape(dps, mps, -1),
            grad_heads.reshape(2, dps, mps, hcols).transpose(1, 2, 0, 3).reshape(dps, mps, -1),
        ],
        axis=2,
    )
    grad_small = jnp.pad(grad_small, ((0, 0), (0, 0), (0, width - grad_small.shape[2])))
    grad_small = grad_small.reshape(dps, xs, cs, width).transpose(2, 1, 0, 3)
    grad_small = scatter_axis(scatter_axis(grad_small, "c"), "x")
    def scatter_data(pieces):
        pieces = pieces.reshape((zs, ys) + pieces.shape[1:]).swapaxes(0, 1)
        return scatter_axis(scatter_axis(pieces, "y"), "z")

    grad_qo = jnp.concatenate(
        [
            grad_query.reshape(dps, drows, width).astype(bf),
            grad_out.reshape(dps, drows, width).astype(bf),
        ],
        axis=1,
    )
    sums_qo = scatter_data(after(grad_qo, by_block, sum_down_own))
    sum_query, sum_out = sums_qo[:drows], sums_qo[drows:].T
    grad_pack = jnp.concatenate(
        [
            grad_keyval[:, :, :width].astype(bf),
            grad_keyval[:, :, width:].astype(bf),
            jnp.pad(grad_small[:, None].astype(bf), ((0, 0), (0, 15), (0, 0))),
        ],
        axis=1,
    )
    sums_pack = scatter_data(after(grad_pack, sum_gateup3))
    sum_gateup = sum_gateup3.astype(fl) + gateup_d
    sum_keyval = jnp.concatenate([sums_pack[:krows], sums_pack[kpad : kpad + krows]], axis=1)
    sum_small = sums_pack[2 * kpad]
    sum_layers = sum_small[: 4 * gcols].reshape(4, gcols)
    sum_heads = sum_small[4 * gcols : 4 * gcols + 2 * hcols].reshape(2, hcols)

    masters = (w_query, w_keyval, w_out, w_gateup, w_down, gain_layers, gain_heads)
    sums = (sum_query, sum_keyval, sum_out, sum_gateup, sum_down, sum_layers, sum_heads)
    totals = tuple((item * norm_factor for item in sums))
    moms = (mom_query, mom_keyval, mom_out, mom_gateup, mom_down, mom_layers, mom_heads)
    varis = (var_query, var_keyval, var_out, var_gateup, var_down, var_layers, var_heads)
    decays = (DECAY, DECAY, DECAY, DECAY, DECAY, 0.0, 0.0)
    updated = [
        adam_update(master, mom, var, grad, decay)
        for master, mom, var, grad, decay in zip(masters, moms, varis, totals, decays)
    ]
    return (
        (block_out, grad_input)
        + totals
        + tuple(item[0] for item in updated)
        + tuple(item[1] for item in updated)
        + tuple(item[2] for item in updated)
    )


def solution(mesh):
    dps, mps = mesh.shape["dp"], mesh.shape["mp"]
    zs = 4 if dps % 4 == 0 else 1
    cs = 2 if mps % 2 == 0 else 1
    split = Mesh(mesh.devices.reshape(zs, dps // zs, mps // cs, cs), ("z", "y", "x", "c"))
    mp = ("x", "c")
    both = DP + mp
    weights = (
        P(DP, mp),
        P(both, None),
        P(mp, DP),
        P(None, DP, mp),
        P(mp, DP),
        P(None, both),
        P(None, both),
    )
    tokens = P(DP, None)
    states = tuple(spec for spec in weights for _ in range(2))
    in_specs = (tokens, tokens, P()) + weights + states
    out_specs = (tokens, tokens) + weights * 4
    return jax.shard_map(
        on_device, mesh=split, in_specs=in_specs, out_specs=out_specs, check_vma=False
    )
```

```python
import functools

import jax
import jax.numpy as jnp
import numpy as np
from jax import lax
from jax.experimental import pallas as pl
from jax.experimental.pallas import tpu as pltpu
from jax.sharding import Mesh, PartitionSpec as P

HD = 256
SEQ = 2048
ADAM_STEP = 4


EPS = 1e-06
THETA = 1000000.0
LEARN = 0.02
BETA_ONE = 0.9
BETA_TWO = 0.95
ADAM_EPS = 1e-08
DECAY = 0.1
GELU_COEF = 0.7978845608028654
GELU_CUBE = 0.044715
NEG_FILL = -1e30

bf = jnp.bfloat16
fl = jnp.float32
DP = ("z", "y")


def rms_scale(values):
    return lax.rsqrt(jnp.mean(values * values, axis=-1, keepdims=True) + EPS)


def norm_back(values, scale, factor, incoming):
    scaled = incoming * factor
    return scale * (
        scaled - values * (scale * scale) * jnp.mean(scaled * values, axis=-1, keepdims=True)
    )


def rotate_half(values):
    middle = values.shape[-1] // 2
    return jnp.concatenate([-values[..., middle:], values[..., :middle]], axis=-1)


def rope_tables(position, width):
    middle = width // 2
    freqs = THETA ** (-2.0 * jnp.arange(middle, dtype=jnp.float32) / width)
    angle = position.astype(jnp.float32)[:, None] * freqs[None, :]
    cosine = jnp.concatenate([jnp.cos(angle), jnp.cos(angle)], axis=-1)
    sine = jnp.concatenate([jnp.sin(angle), jnp.sin(angle)], axis=-1)
    return (cosine, sine)


def gelu_parts(values):
    inner = GELU_COEF * (values + GELU_CUBE * values * values * values)
    tanh_val = jnp.tanh(inner)
    value = 0.5 * values * (1.0 + tanh_val)
    slope = 0.5 * (1.0 + tanh_val) + 0.5 * values * (1.0 - tanh_val * tanh_val) * GELU_COEF * (
        1.0 + 3.0 * GELU_CUBE * values * values
    )
    return (value, slope)


def adam_update(weight, mom, var, grad, decay):
    mom_new = BETA_ONE * mom + (1.0 - BETA_ONE) * grad
    var_new = BETA_TWO * var + (1.0 - BETA_TWO) * grad * grad
    fix_one = 1.0 - BETA_ONE**ADAM_STEP
    fix_two = 1.0 - BETA_TWO**ADAM_STEP
    direction = mom_new / fix_one / (jnp.sqrt(var_new / fix_two) + ADAM_EPS)
    return (weight - LEARN * (direction + decay * weight), mom_new, var_new)


def rotated(value, axis, by):
    size = lax.axis_size(axis)
    return lax.ppermute(value, axis, [(i, (i + by) % size) for i in range(size)])


def shifted(value, by):
    size = lax.axis_size(DP)
    return lax.ppermute(
        value, DP, [(i, i + by) for i in range(size) if 0 <= i + by < size]
    )


def pick(value, index):
    return lax.dynamic_index_in_dim(value, index, 0, keepdims=False)


def gather_axis(value, axis):
    size = lax.axis_size(axis)
    me = lax.axis_index(axis)
    if size == 2:
        other = rotated(value, axis, 1)
        return jnp.stack([jnp.where(me == 0, value, other), jnp.where(me == 0, other, value)])
    whole = jnp.zeros((size,) + value.shape, value.dtype)
    whole = lax.dynamic_update_index_in_dim(whole, value, me, 0)
    for by in range(1, size):
        whole = lax.dynamic_update_index_in_dim(
            whole, rotated(value, axis, by), (me - by) % size, 0
        )
    return whole


def scatter_axis(pieces, axis):
    size = lax.axis_size(axis)
    me = lax.axis_index(axis)
    total = pick(pieces, me).astype(fl)
    for by in range(1, size):
        sent = pick(pieces, (me + by) % size).astype(bf)
        total = total + rotated(sent, axis, by).astype(fl)
    return total


def by_dp_axis(pieces, zs, ys):
    return pieces.reshape((zs, ys) + pieces.shape[1:]).swapaxes(0, 1)


def scatter_model(partial, *gates):
    xs, cs = lax.axis_size("x"), lax.axis_size("c")
    rows, width = partial.shape
    view = partial.reshape(xs, cs, rows // (xs * cs), width)
    half = after(scatter_axis(view.swapaxes(0, 1), "c"), *gates)
    return scatter_axis(half, "x")


def gather_model(part, *gates):
    return gather_core(after(gather_axis(part, "x"), *gates))


def gather_core(both):
    four = gather_axis(both, "c").swapaxes(0, 1)
    return four.reshape((-1,) + both.shape[2:])


def ring_index(index, size):
    return index ^ (index >> 1) if size == 4 else index


def ring_step(value):
    size = lax.axis_size("z")
    pairs = [(ring_index(i, size), ring_index((i + 1) % size, size)) for i in range(size)]
    return lax.ppermute(value, "z", pairs)


def ring_source(back):
    size = lax.axis_size("z")
    place = ring_index(lax.axis_index("z"), size)
    return ring_index((place - back + size) % size, size)


def after(value, *others):
    return lax.optimization_barrier((value,) + others)[0]


def over_y(value):
    return [rotated(value, "y", by) for by in range(1, lax.axis_size("y"))]


def in_order(blocks):
    zs, ys = lax.axis_size("z"), lax.axis_size("y")
    me = lax.axis_index("y")
    whole = jnp.zeros((zs * ys,) + blocks[0][0].shape, blocks[0][0].dtype)
    for step, row in enumerate(blocks):
        source = ring_source(step)
        for by, piece in enumerate(row):
            whole = lax.dynamic_update_index_in_dim(
                whole, piece, source * ys + (me - by) % ys, 0
            )
    return whole


TILE = 256
NOMINAL = pl.CostEstimate(flops=1, bytes_accessed=1, transcendentals=0)


def _columns(block, index, valid):
    at = index * TILE + lax.broadcasted_iota(jnp.int32, block.shape, 1)
    return jnp.where(at < valid, block, jnp.zeros_like(block))


def _flat(block):
    return block.reshape(-1, block.shape[-1])


def _hidden_kernel(valid, mid_ref, w_ref, hid_ref, gate_ref, up_ref):
    mid = mid_ref[...]
    gate = jnp.dot(mid, _flat(w_ref[:, 0]), preferred_element_type=fl)
    up = jnp.dot(mid, _flat(w_ref[:, 1]), preferred_element_type=fl)
    value, slope = gelu_parts(gate)
    hid_ref[...] = (value * up).astype(bf)
    gate_ref[...] = (up * slope).astype(bf)
    up_ref[...] = value.astype(bf)


def _down_kernel(valid, hid_ref, down_ref, out_ref):
    index = pl.program_id(0)

    def add(hid, down):
        part = lax.dot_general(hid, down, (((1,), (1,)), ((), ())), preferred_element_type=fl)

        @pl.when(index == 0)
        def _():
            out_ref[...] = part

        @pl.when(index > 0)
        def _():
            out_ref[...] += part

    last = index == pl.num_programs(0) - 1

    @pl.when(jnp.logical_not(last))
    def _():
        add(hid_ref[...], _flat(down_ref[:, 0]))

    @pl.when(last)
    def _():
        add(_columns(hid_ref[...], index, valid), _columns(_flat(down_ref[:, 0]), index, valid))


def _backward_kernel(valid, ffn_ref, gate_ref, up_ref, w_ref, down_ref, mid_ref, ggate_ref, gup_ref):
    index = pl.program_id(0)
    grad = jnp.dot(ffn_ref[...], _flat(down_ref[:, 0]), preferred_element_type=fl)
    ggate = (grad * gate_ref[...].astype(fl)).astype(bf)
    gup = (grad * up_ref[...].astype(fl)).astype(bf)
    ggate_ref[...] = ggate
    gup_ref[...] = gup

    def add(one, two, w_one, w_two):
        dims = (((1,), (1,)), ((), ()))
        part = lax.dot_general(one, w_one, dims, preferred_element_type=fl)
        part = part + lax.dot_general(two, w_two, dims, preferred_element_type=fl)

        @pl.when(index == 0)
        def _():
            mid_ref[...] = part

        @pl.when(index > 0)
        def _():
            mid_ref[...] += part

    last = index == pl.num_programs(0) - 1
    w_one, w_two = _flat(w_ref[:, 0]), _flat(w_ref[:, 1])

    @pl.when(jnp.logical_not(last))
    def _():
        add(ggate, gup, w_one, w_two)

    @pl.when(last)
    def _():
        add(
            _columns(ggate, index, valid),
            _columns(gup, index, valid),
            _columns(w_one, index, valid),
            _columns(w_two, index, valid),
        )


def _grads_kernel(pairs, left_ref, *refs):
    turned = refs[-1]

    @pl.when(pl.program_id(0) == 0)
    def _():
        turned[...] = left_ref[...].T

    for right_ref, out_ref in zip(refs[:pairs], refs[pairs : 2 * pairs]):
        grads = jnp.dot(turned[...], right_ref[...], preferred_element_type=fl).astype(bf)
        out_ref[...] = grads.reshape(out_ref.shape)


def grads_call(left, rights, pieces, name):
    rows, depth = left.shape
    units = rights[0].shape[1]
    split = pieces if depth // pieces % 16 == 0 else 1
    shape = (split, depth // split, units)
    column = pl.BlockSpec((rows, TILE), lambda j: (0, j))
    out = pl.BlockSpec(shape[:2] + (TILE,), lambda j: (0, 0, j))
    results = pl.pallas_call(
        functools.partial(_grads_kernel, len(rights)),
        out_shape=[jax.ShapeDtypeStruct(shape, bf)] * len(rights),
        grid=(pl.cdiv(units, TILE),),
        in_specs=[pl.BlockSpec((rows, depth), lambda j: (0, 0))] + [column] * len(rights),
        out_specs=[out] * len(rights),
        scratch_shapes=[pltpu.VMEM((depth, rows), bf)],
        compiler_params=pltpu.CompilerParams(
            dimension_semantics=("arbitrary",), vmem_limit_bytes=40 * 1024 * 1024
        ),
        cost_estimate=NOMINAL,
        name=name,
    )(left, *rights)
    return [result.reshape(pieces, depth // pieces, units) for result in results]


def ffn_call(kernel, name, rows, lefts, weights, tiles_in, total, tiles_out):
    units = weights[0].shape[-1]
    depth = weights[0].shape[0] * weights[0].shape[2]
    kinds = sum(w.shape[1] for w in weights)
    column = pl.BlockSpec((rows, TILE), lambda j: (0, j))
    whole = pl.BlockSpec((rows, depth), lambda j: (0, 0))
    tile = jax.ShapeDtypeStruct((rows, units), bf)
    return pl.pallas_call(
        functools.partial(kernel, units),
        out_shape=[jax.ShapeDtypeStruct((rows, depth), fl)] * total + [tile] * tiles_out,
        grid=(pl.cdiv(units, TILE),),
        in_specs=[whole] * len(lefts)
        + [column] * len(tiles_in)
        + [pl.BlockSpec(w.shape[:3] + (TILE,), lambda j: (0, 0, 0, j)) for w in weights],
        out_specs=[whole] * total + [column] * tiles_out,
        compiler_params=pltpu.CompilerParams(
            dimension_semantics=("arbitrary",), vmem_limit_bytes=40 * 1024 * 1024
        ),
        cost_estimate=NOMINAL,
        name=name,
    )(*lefts, *tiles_in, *weights)


HALVES = 2


def row_call(kernel, name, rows, by_rows, whole, out_rows, out_whole=(), scratch=()):
    step = rows // HALVES

    def cut(shape):
        return pl.BlockSpec((step,) + shape[1:], lambda i: (i, 0))

    def kept(shape):
        return pl.BlockSpec(shape, lambda i: (0,) * len(shape))

    return pl.pallas_call(
        kernel,
        out_shape=[jax.ShapeDtypeStruct(*item) for item in list(out_rows) + list(out_whole)],
        grid=(HALVES,),
        in_specs=[cut(item.shape) for item in by_rows] + [kept(item.shape) for item in whole],
        out_specs=[cut(item[0]) for item in out_rows] + [kept(item[0]) for item in out_whole],
        scratch_shapes=scratch,
        compiler_params=pltpu.CompilerParams(
            dimension_semantics=("arbitrary",), vmem_limit_bytes=48 * 1024 * 1024
        ),
        cost_estimate=NOMINAL,
        name=name,
    )(*by_rows, *whole)


def _project_kernel(
    x_ref,
    cos_ref,
    sin_ref,
    gain_ref,
    head_ref,
    query_ref,
    keyval_ref,
    normed_ref,
    scale_ref,
    qraw_ref,
    qscale_ref,
    qrot_ref,
    kraw_ref,
    kscale_ref,
    kv_ref,
):
    width = qraw_ref.shape[1]
    values = x_ref[...]
    scale = rms_scale(values)
    scale_ref[...] = scale
    normed = (values * scale * gain_ref[...]).astype(bf)
    normed_ref[...] = normed
    cosine, sine = cos_ref[...], sin_ref[...]

    def turned(raw, scale, factor):
        norm = raw * scale * factor
        return (norm * cosine + rotate_half(norm) * sine).astype(bf)

    raw = jnp.dot(normed, query_ref[...], preferred_element_type=fl)
    scale = rms_scale(raw)
    qraw_ref[...] = raw
    qscale_ref[...] = scale
    qrot_ref[...] = turned(raw, scale, head_ref[0:1])
    raw = jnp.dot(normed, keyval_ref[...], preferred_element_type=fl)
    key = raw[:, :width]
    scale = rms_scale(key)
    kraw_ref[...] = key
    kscale_ref[...] = scale
    kv_ref[:, :width] = turned(key, scale, head_ref[1:2])
    kv_ref[:, width:] = raw[:, width:].astype(bf)


ACROSS = (((1,), (1,)), ((), ()))


def _masked_scores(query, keys, low, high, factor):
    scores = lax.dot_general(query, keys, ACROSS, preferred_element_type=fl) * factor
    at = lax.broadcasted_iota(jnp.int32, scores.shape, 1)
    return jnp.where((at >= low) & (at <= high), scores, NEG_FILL)


def _attend_kernel(
    factor, query_ref, low_ref, high_ref, window_ref, out_ref, att_ref, log_ref, part_ref
):
    width = query_ref.shape[1]
    masked = _masked_scores(
        query_ref[...], window_ref[:, :width], low_ref[...], high_ref[...], factor
    )
    top = jnp.max(masked, axis=-1, keepdims=True)
    powers = jnp.exp(masked - top)
    total = jnp.sum(powers, axis=-1, keepdims=True)
    log_ref[...] = top + jnp.log(total)
    probs = (powers * (1.0 / total)).astype(bf)
    attended = jnp.dot(probs, window_ref[:, width:], preferred_element_type=fl).astype(bf)
    att_ref[...] = attended
    part_ref[...] = lax.dot_general(attended, out_ref[...], ACROSS, preferred_element_type=fl)


def _attend_back_kernel(
    factor,
    grad_ref,
    query_ref,
    low_ref,
    high_ref,
    log_ref,
    att_ref,
    qraw_ref,
    qscale_ref,
    cos_ref,
    sin_ref,
    head_ref,
    window_ref,
    out_ref,
    lowq_ref,
    gqin_ref,
    part_ref,
    gkv_ref,
    ghead_ref,
    turned,
):
    width = query_ref.shape[1]
    keys, values = window_ref[:, :width], window_ref[:, width:]
    query = query_ref[...]
    grad_att = jnp.dot(grad_ref[...], out_ref[...], preferred_element_type=fl).astype(bf)
    delta = jnp.sum(
        grad_att.astype(fl) * att_ref[...].astype(fl), axis=-1, keepdims=True
    )
    masked = _masked_scores(query, keys, low_ref[...], high_ref[...], factor)
    probs = jnp.exp(masked - log_ref[...])
    grad_probs = lax.dot_general(grad_att, values, ACROSS, preferred_element_type=fl)
    grad_scores = (probs * (grad_probs - delta) * factor).astype(bf)
    grad_q = jnp.dot(grad_scores, keys, preferred_element_type=fl)
    grad_k = jnp.dot(query.T, grad_scores, preferred_element_type=fl)
    grad_v = jnp.dot(grad_att.T, probs.astype(bf), preferred_element_type=fl)
    back = grad_q * cos_ref[...] - rotate_half(grad_q * sin_ref[...])
    raw, scale = qraw_ref[...], qscale_ref[...]
    gqin = norm_back(raw, scale, head_ref[0:1], back).astype(bf)
    gqin_ref[...] = gqin
    part_ref[...] = lax.dot_general(gqin, lowq_ref[...], ACROSS, preferred_element_type=fl)
    ghead = jnp.sum(back * raw * scale, axis=0, keepdims=True)
    first = pl.program_id(0) == 0

    @pl.when(first)
    def _():
        turned[:width] = grad_k
        turned[width:] = grad_v
        ghead_ref[...] = ghead

    @pl.when(jnp.logical_not(first))
    def _():
        turned[:width] += grad_k
        turned[width:] += grad_v
        ghead_ref[...] += ghead

    @pl.when(pl.program_id(0) == pl.num_programs(0) - 1)
    def _():
        gkv_ref[...] = turned[...].astype(bf).T


def whole_call(kernel, name, ins, outs):
    def kept(shape):
        return pl.BlockSpec(shape, lambda i: (0,) * len(shape))

    return pl.pallas_call(
        kernel,
        out_shape=[jax.ShapeDtypeStruct(*item) for item in outs],
        grid=(1,),
        in_specs=[kept(item.shape) for item in ins],
        out_specs=[kept(item[0]) for item in outs],
        compiler_params=pltpu.CompilerParams(
            dimension_semantics=("arbitrary",), vmem_limit_bytes=48 * 1024 * 1024
        ),
        cost_estimate=NOMINAL,
        name=name,
    )(*ins)


def _input_back_kernel(parts, *refs):
    cos_ref, sin_ref, raw_ref, scale_ref, head_ref, low_ref = refs[parts : parts + 6]
    (
        normed_ref,
        in_ref,
        scale_in_ref,
        resid_grad_ref,
        attn_ref,
        scale_attn_ref,
        mid_grad_ref,
        resid_ref,
        scale_mid_ref,
        out_grad_ref,
        ffn_ref,
        scale_ffn_ref,
        gain_ref,
        gkv_ref,
        ghead_ref,
        grad_ref,
        layers_ref,
    ) = refs[parts + 6 :]
    width = raw_ref.shape[1]
    total = refs[0][...]
    for ref in refs[1:parts]:
        total = total + ref[...].astype(fl)
    grad = total[:, :width]
    back = grad * cos_ref[...] - rotate_half(grad * sin_ref[...])
    raw, scale = raw_ref[...], scale_ref[...]
    gkv_ref[:, :width] = norm_back(raw, scale, head_ref[1:2], back).astype(bf)
    gkv_ref[:, width:] = total[:, width:].astype(bf)
    ghead_ref[...] = jnp.sum(back * raw * scale, axis=0, keepdims=True)
    part = lax.dot_general(gkv_ref[...], low_ref[...], ACROSS, preferred_element_type=fl)
    normed = normed_ref[...] + part
    values, scale, resid_grad = in_ref[...], scale_in_ref[...], resid_grad_ref[...]
    grad_ref[...] = (resid_grad + norm_back(values, scale, gain_ref[0:1], normed)).astype(bf)

    def over_rows(item):
        return jnp.sum(item, axis=0, keepdims=True)

    layers_ref[0:1] = over_rows(normed * values * scale)
    layers_ref[1:2] = over_rows(resid_grad * attn_ref[...] * scale_attn_ref[...])
    layers_ref[2:3] = over_rows(mid_grad_ref[...] * resid_ref[...] * scale_mid_ref[...])
    layers_ref[3:4] = over_rows(out_grad_ref[...] * ffn_ref[...] * scale_ffn_ref[...])


def on_device(
    block_in,
    out_grad,
    segment_ids,
    w_query,
    w_keyval,
    w_out,
    w_gateup,
    w_down,
    gain_layers,
    gain_heads,
    mom_query,
    var_query,
    mom_keyval,
    var_keyval,
    mom_out,
    var_out,
    mom_gateup,
    var_gateup,
    mom_down,
    var_down,
    mom_layers,
    var_layers,
    mom_heads,
    var_heads,
):
    zs, ys = lax.axis_size("z"), lax.axis_size("y")
    xs, cs = lax.axis_size("x"), lax.axis_size("c")
    dps, mps = zs * ys, xs * cs
    model = lax.axis_index("x") * cs + lax.axis_index("c")
    device = lax.axis_index("z") * ys + lax.axis_index("y")
    width = HD
    rows, depth = block_in.shape
    quarter = rows // mps
    factor = width ** (-0.5)
    norm_factor = float(rows * dps) ** (-0.5)
    drows = w_query.shape[0]
    krows = w_keyval.shape[0]
    gcols, hcols = gain_layers.shape[1], gain_heads.shape[1]

    kpad = -(-krows // 16) * 16
    small = jnp.concatenate([gain_layers.reshape(-1), gain_heads.reshape(-1)]).astype(bf)
    small = jnp.pad(small, (0, width - small.shape[0])).reshape(1, width)
    fill = jnp.zeros((kpad - krows, width), bf)
    pack = jnp.concatenate(
        [
            w_query.astype(bf),
            w_keyval[:, :width].astype(bf),
            fill,
            w_keyval[:, width:].astype(bf),
            fill,
            jnp.pad(small, ((0, 15), (0, 0))),
        ],
        axis=0,
    )
    by_z = gather_axis(pack, "z")
    by_dp = gather_axis(by_z, "y").swapaxes(0, 1).reshape((dps,) + pack.shape)
    low_query = by_dp[:, :drows].reshape(depth, width)
    kv_mine = by_dp[:, drows:]

    gateup0, down0 = w_gateup.astype(bf), w_down.T.astype(bf)
    gateup1 = ring_step(after(gateup0, by_z))
    gateup0_y = over_y(after(gateup0, by_dp))
    gateup2 = ring_step(gateup1)
    gateup1_y = over_y(after(gateup1, *gateup0_y))
    gateup3 = ring_step(gateup2)
    down_y = over_y(after(down0, *gateup1_y))

    kv_all = gather_axis(gather_axis(after(kv_mine, gateup1), "x"), "c")
    kv_all = after(kv_all, gateup2, *gateup0_y)
    lanes = np.arange(cs * xs * dps * kpad).reshape(cs, xs, dps, kpad)
    core, xx, dd, rr = np.unravel_index(lanes.reshape(-1), lanes.shape)
    owner = np.where(rr < krows, (dd * mps + xx * cs + core) * krows + rr, -1)
    depth_index = jnp.arange(depth, dtype=jnp.int32)
    sorter = (depth_index[:, None] == jnp.asarray(owner, jnp.int32)[None, :]).astype(bf)
    kv_pad = jnp.concatenate(
        [
            kv_all[:, :, :, :kpad].reshape(-1, width),
            kv_all[:, :, :, kpad : 2 * kpad].reshape(-1, width),
        ],
        axis=1,
    )
    low_keyval = jnp.dot(sorter, kv_pad, preferred_element_type=fl).astype(bf)
    low_keyval = after(low_keyval, gateup3, *gateup1_y)
    mine = np.arange(dps * kpad)
    owner = (mine // kpad) * mps * krows + mine % kpad
    owner = jnp.asarray(owner, jnp.int32) + model * krows
    chooser = (depth_index[:, None] == owner[None, :]) & jnp.asarray(mine % kpad < krows)[None, :]
    gains = kv_all[:, :, :, 2 * kpad].astype(fl)
    gain_scale = 1.0 + gains[:, :, :, : 4 * gcols].reshape(cs, xs, dps, 4, gcols).transpose(
        3, 2, 1, 0, 4
    ).reshape(4, depth)
    head_scale = 1.0 + gains[:, :, :, 4 * gcols : 4 * gcols + 2 * hcols].reshape(
        cs, xs, dps, 2, hcols
    ).transpose(3, 2, 1, 0, 4).reshape(2, width)

    margin = SEQ // 2
    first_row = device * rows
    shifted_first = first_row + margin
    seq_start = shifted_first // SEQ * SEQ
    span = SEQ // rows
    position = shifted_first + jnp.arange(rows, dtype=jnp.int32)
    cosine, sine = rope_tables(position % SEQ, width)

    def part_rows(values):
        return lax.dynamic_slice_in_dim(values, model * quarter, quarter, 0)

    (
        normed_in,
        scale_in,
        query_raw,
        scale_query,
        query_rot,
        key_raw,
        scale_key,
        keyval_low,
    ) = row_call(
        _project_kernel,
        "project",
        rows,
        [block_in, cosine, sine],
        [gain_scale[0:1], head_scale, low_query, low_keyval],
        [
            ((rows, depth), bf),
            ((rows, 1), fl),
            ((rows, width), fl),
            ((rows, 1), fl),
            ((rows, width), bf),
            ((rows, width), fl),
            ((rows, 1), fl),
            ((rows, 2 * width), bf),
        ],
    )
    sent_kv = after(part_rows(keyval_low), *down_y)
    earlier = jnp.stack([shifted(sent_kv, by) for by in range(span - 1, 0, -1)])
    out_by_z = gather_axis(after(w_out.T.astype(bf), sent_kv), "z")
    low_out = gather_axis(out_by_z, "y").swapaxes(0, 1).reshape(depth, width)
    down0 = after(jnp.stack([down0] + down_y), earlier, out_by_z)
    down1 = ring_step(down0)
    gateup2_y = over_y(after(gateup2, earlier, low_out))
    four = gather_axis(gather_axis(earlier, "x"), "c")
    earlier = four.transpose(2, 1, 0, 3, 4).reshape((span - 1) * rows, 2 * width)
    earlier = after(earlier, down1, *gateup2_y)
    window = jnp.concatenate([earlier, keyval_low], axis=0)
    reach = span * rows
    window_first = first_row + rows - reach
    seg_query = lax.dynamic_slice_in_dim(segment_ids, first_row, rows, 0)
    doc_first = jnp.sum(
        (segment_ids[None, :] < seg_query[:, None]).astype(jnp.int32), axis=1, keepdims=True
    )
    run_first = jnp.maximum(doc_first, seq_start - margin) - window_first
    run_last = jnp.arange(rows, dtype=jnp.int32)[:, None] + (reach - rows)
    attended, log_total, attn_part = row_call(
        functools.partial(_attend_kernel, factor),
        "attend",
        rows,
        [query_rot, run_first, run_last],
        [window, low_out],
        [((rows, width), bf), ((rows, 1), fl), ((rows, depth), fl)],
    )
    down2 = ring_step(down1)
    gateup3_y = over_y(after(gateup3, *gateup2_y))

    in_part, scale_in_part = part_rows(block_in), part_rows(scale_in)
    grad_part = part_rows(out_grad)
    attn_proj = after(scatter_model(attn_part), down2, *gateup3_y)
    down3 = ring_step(down2)
    scale_attn = rms_scale(attn_proj)
    resid = in_part + attn_proj * scale_attn * gain_scale[1]
    scale_mid = rms_scale(resid)
    normed_mid = gather_model((resid * scale_mid * gain_scale[2]).astype(bf))
    low_gateup = in_order(
        [
            [gateup0] + gateup0_y,
            [gateup1] + gateup1_y,
            [gateup2] + gateup2_y,
            [gateup3] + gateup3_y,
        ]
    )
    low_down = in_order([[block[by] for by in range(ys)] for block in (down0, down1, down2, down3)])
    low_down = low_down[:, None]
    if drows % 16:
        low_gateup = low_gateup.swapaxes(0, 1).reshape((1, 2, depth, -1))
        low_down = low_down.reshape((1, 1, depth, -1))
    hidden, gate_factor, up_factor = ffn_call(
        _hidden_kernel, "ffn_hidden", rows, [normed_mid], [low_gateup], [], 0, 3
    )
    (ffn_part,) = ffn_call(_down_kernel, "ffn_down", rows, [], [low_down], [hidden], 1, 0)
    ffn_proj = scatter_model(ffn_part)
    scale_ffn = rms_scale(ffn_proj)
    grad_ffn = gather_model(norm_back(ffn_proj, scale_ffn, gain_scale[3], grad_part).astype(bf))
    (grad_down,) = grads_call(grad_ffn, [hidden], dps, "down_grads")
    grad_down = grad_down.reshape((zs, ys) + grad_down.shape[1:])
    sum_down1 = ring_step(pick(grad_down, ring_source(1)))
    grad_ffn = after(grad_ffn, grad_down)
    mid_part, grad_gate, grad_up = ffn_call(
        _backward_kernel,
        "ffn_backward",
        rows,
        [grad_ffn],
        [low_gateup, low_down],
        [gate_factor, up_factor],
        1,
        2,
    )
    mid_part = after(mid_part, sum_down1)
    grads_gateup = grads_call(normed_mid, [grad_gate, grad_up], dps, "gateup_grads")

    def gateup_piece(target, by):
        index = ring_source(target) * ys + (lax.axis_index("y") + by) % ys
        return jnp.stack([pick(item, index) for item in grads_gateup])

    def gateup_over_y(target, *gates):
        return [
            rotated(after(gateup_piece(target, by), *gates), "y", by) for by in range(1, ys)
        ]

    def gateup_add(came, target, over):
        total = gateup_piece(target, 0).astype(fl)
        for item in ([] if came is None else [came]) + over:
            total = total + item.astype(fl)
        return total

    def down_add(came, target):
        return came.astype(fl) + pick(grad_down, ring_source(target)).astype(fl)

    over_a = gateup_over_y(1)
    over_b = gateup_over_y(2, *over_a)
    down_two = down_add(sum_down1, 2).astype(bf)
    sum_down2 = ring_step(down_two)
    grad_mid = after(scatter_model(mid_part, down_two), sum_down2, *over_a)
    down_three = down_add(sum_down2, 3).astype(bf)
    sum_down3 = ring_step(down_three)
    grad_resid = grad_part + norm_back(resid, scale_mid, gain_scale[2], grad_mid)
    grad_attn = gather_axis(
        norm_back(attn_proj, scale_attn, gain_scale[1], grad_resid).astype(bf), "x"
    )
    grad_attn = gather_core(after(grad_attn, sum_down3, *over_b))
    gateup_one = gateup_add(None, 1, [after(item, sum_down3) for item in over_a]).astype(bf)
    sum_gateup1 = ring_step(gateup_one)
    over_c = gateup_over_y(3, *over_b)
    grad_attn = after(grad_attn, gateup_one)
    grad_out = jnp.einsum("td,tc->dc", grad_attn, attended, preferred_element_type=fl)
    grad_qin, normed_part, grad_seq, grad_qhead = row_call(
        functools.partial(_attend_back_kernel, factor),
        "attend_back",
        rows,
        [
            grad_attn,
            query_rot,
            run_first,
            run_last,
            log_total,
            attended,
            query_raw,
            scale_query,
            cosine,
            sine,
        ],
        [head_scale, window, low_out, low_query],
        [((rows, width), bf), ((rows, depth), fl)],
        [((reach, 2 * width), bf), ((1, width), fl)],
        [pltpu.VMEM((2 * width, reach), fl)],
    )
    grad_query = jnp.einsum("td,tc->dc", normed_in, grad_qin, preferred_element_type=fl)
    grad_qo = jnp.concatenate(
        [
            grad_query.reshape(dps, drows, width).astype(bf),
            grad_out.reshape(dps, drows, width).astype(bf),
        ],
        axis=1,
    )
    qo_over_y = scatter_axis(by_dp_axis(after(grad_qo, *over_c), zs, ys), "y").astype(bf)
    grad_seq = after(grad_seq, sum_gateup1, *over_c)
    gateup_two = gateup_add(sum_gateup1, 2, over_b).astype(bf)
    sum_gateup2 = ring_step(gateup_two)
    by_model = grad_seq.reshape(span, xs, cs, quarter, 2 * width).transpose(2, 1, 0, 3, 4)
    over_d = gateup_over_y(4, qo_over_y)
    by_block = after(scatter_axis(by_model, "c"), gateup_two)
    own, own_z = lax.axis_index("y"), lax.axis_index("z")
    qo_over_z = [
        rotated(pick(qo_over_y, (own_z + by) % zs), "z", by) for by in range(1, zs)
    ]
    by_block = after(scatter_axis(by_block, "x"), sum_gateup2, *over_d, *qo_over_z)
    grad_kparts = [by_block[span - 1]] + [
        shifted(by_block[span - 1 - by].astype(bf), -by) for by in range(1, span)
    ]
    gateup_three = gateup_add(after(sum_gateup2, *grad_kparts), 3, over_c).astype(bf)
    gateup_three = [gateup_three[i] for i in range(2)]
    sum_gateup3 = [ring_step(gateup_three[0])]
    sum_gateup3.append(ring_step(after(gateup_three[1], *sum_gateup3)))
    grad_kparts[0] = after(grad_kparts[0], *gateup_three)

    sum_down = down_add(after(sum_down3, by_block), 4)
    down_over_y = [
        rotated(after(pick(sum_down, (own + by) % ys).astype(bf), *grad_kparts), "y", by)
        for by in range(1, ys)
    ]

    ffn_late = after(ffn_proj, grad_seq)
    out_part = (resid + ffn_late * scale_ffn * gain_scale[3]).astype(bf)
    block_out = gather_model(after(out_part, by_block)).astype(fl)

    cos_part, sin_part = part_rows(cosine), part_rows(sine)
    key_part, scale_kpart = part_rows(key_raw), part_rows(scale_key)
    grad_kvin, grad_khead, grad_in_part, grad_layers = whole_call(
        functools.partial(_input_back_kernel, span),
        "input_back",
        grad_kparts
        + [cos_part, sin_part, key_part, scale_kpart, head_scale, low_keyval]
        + [
            scatter_model(normed_part),
            in_part,
            scale_in_part,
            grad_resid,
            attn_proj,
            scale_attn,
            grad_mid,
            resid,
            scale_mid,
            grad_part,
            ffn_proj,
            scale_ffn,
            gain_scale,
        ],
        [((quarter, 2 * width), bf), ((1, width), fl), ((quarter, depth), bf), ((4, depth), fl)],
    )
    normed_mine = jnp.dot(after(normed_in, grad_seq), chooser.astype(bf), preferred_element_type=fl).astype(bf)
    grad_keyval = jnp.einsum(
        "td,tc->dc", normed_mine, gather_model(grad_kvin, sum_gateup3[0], *down_over_y), preferred_element_type=fl
    ).reshape(dps, kpad, 2 * width)

    grad_input = gather_model(grad_in_part).astype(fl)
    grad_heads = jnp.concatenate([grad_qhead, grad_khead], axis=0)
    grad_small = jnp.concatenate(
        [
            grad_layers.reshape(4, dps, mps, gcols).transpose(1, 2, 0, 3).reshape(dps, mps, -1),
            grad_heads.reshape(2, dps, mps, hcols).transpose(1, 2, 0, 3).reshape(dps, mps, -1),
        ],
        axis=2,
    )
    grad_small = jnp.pad(grad_small, ((0, 0), (0, 0), (0, width - grad_small.shape[2])))
    grad_small = grad_small.reshape(dps, xs, cs, width).transpose(2, 1, 0, 3)
    grad_small = scatter_axis(scatter_axis(grad_small, "c"), "x")
    grad_pack = jnp.concatenate(
        [
            grad_keyval[:, :, :width].astype(bf),
            grad_keyval[:, :, width:].astype(bf),
            jnp.pad(grad_small[:, None].astype(bf), ((0, 0), (0, 15), (0, 0))),
        ],
        axis=1,
    )
    sums_pack = scatter_axis(by_dp_axis(grad_pack, zs, ys), "y")
    sums_pack = scatter_axis(after(sums_pack, sum_gateup3[1]), "z")
    sums_qo = pick(after(qo_over_y, grad_pack), own_z).astype(fl)
    for item in qo_over_z:
        sums_qo = sums_qo + item.astype(fl)
    sum_query, sum_out = sums_qo[:drows], sums_qo[drows:].T
    sum_gateup = gateup_add(after(jnp.stack(sum_gateup3), grad_pack), 4, over_d)
    sum_down = pick(after(sum_down, grad_pack), own)
    for item in down_over_y:
        sum_down = sum_down + item.astype(fl)
    sum_down = sum_down.T
    sum_keyval = jnp.concatenate([sums_pack[:krows], sums_pack[kpad : kpad + krows]], axis=1)
    sum_small = sums_pack[2 * kpad]
    sum_layers = sum_small[: 4 * gcols].reshape(4, gcols)
    sum_heads = sum_small[4 * gcols : 4 * gcols + 2 * hcols].reshape(2, hcols)

    masters = (w_query, w_keyval, w_out, w_gateup, w_down, gain_layers, gain_heads)
    sums = (sum_query, sum_keyval, sum_out, sum_gateup, sum_down, sum_layers, sum_heads)
    totals = tuple((item * norm_factor for item in sums))
    moms = (mom_query, mom_keyval, mom_out, mom_gateup, mom_down, mom_layers, mom_heads)
    varis = (var_query, var_keyval, var_out, var_gateup, var_down, var_layers, var_heads)
    decays = (DECAY, DECAY, DECAY, DECAY, DECAY, 0.0, 0.0)
    updated = [
        adam_update(master, mom, var, grad, decay)
        for master, mom, var, grad, decay in zip(masters, moms, varis, totals, decays)
    ]
    return (
        (block_out, grad_input)
        + totals
        + tuple(item[0] for item in updated)
        + tuple(item[1] for item in updated)
        + tuple(item[2] for item in updated)
    )


def solution(mesh):
    dps, mps = mesh.shape["dp"], mesh.shape["mp"]
    zs = 4 if dps % 4 == 0 else 1
    cs = 2 if mps % 2 == 0 else 1
    split = Mesh(mesh.devices.reshape(zs, dps // zs, mps // cs, cs), ("z", "y", "x", "c"))
    mp = ("x", "c")
    both = DP + mp
    weights = (
        P(DP, mp),
        P(both, None),
        P(mp, DP),
        P(None, DP, mp),
        P(mp, DP),
        P(None, both),
        P(None, both),
    )
    tokens = P(DP, None)
    states = tuple(spec for spec in weights for _ in range(2))
    in_specs = (tokens, tokens, P()) + weights + states
    out_specs = (tokens, tokens) + weights * 4
    return jax.shard_map(
        on_device, mesh=split, in_specs=in_specs, out_specs=out_specs, check_vma=False
    )
```

```python
import functools

import jax
import jax.numpy as jnp
import numpy as np
from jax import lax
from jax.experimental import pallas as pl
from jax.experimental.pallas import tpu as pltpu
from jax.sharding import Mesh, PartitionSpec as P

HD = 256
SEQ = 2048
ADAM_STEP = 4


EPS = 1e-06
THETA = 1000000.0
LEARN = 0.02
BETA_ONE = 0.9
BETA_TWO = 0.95
ADAM_EPS = 1e-08
DECAY = 0.1
GELU_COEF = 0.7978845608028654
GELU_CUBE = 0.044715
NEG_FILL = -1e30

bf = jnp.bfloat16
fl = jnp.float32
DP = ("z", "y")


def rms_scale(values):
    return lax.rsqrt(jnp.mean(values * values, axis=-1, keepdims=True) + EPS)


def norm_back(values, scale, factor, incoming):
    scaled = incoming * factor
    return scale * (
        scaled - values * (scale * scale) * jnp.mean(scaled * values, axis=-1, keepdims=True)
    )


def rotate_half(values):
    middle = values.shape[-1] // 2
    return jnp.concatenate([-values[..., middle:], values[..., :middle]], axis=-1)


def rope_tables(position, width):
    middle = width // 2
    freqs = THETA ** (-2.0 * jnp.arange(middle, dtype=jnp.float32) / width)
    angle = position.astype(jnp.float32)[:, None] * freqs[None, :]
    cosine = jnp.concatenate([jnp.cos(angle), jnp.cos(angle)], axis=-1)
    sine = jnp.concatenate([jnp.sin(angle), jnp.sin(angle)], axis=-1)
    return (cosine, sine)


def gelu_parts(values):
    inner = GELU_COEF * (values + GELU_CUBE * values * values * values)
    tanh_val = jnp.tanh(inner)
    value = 0.5 * values * (1.0 + tanh_val)
    slope = 0.5 * (1.0 + tanh_val) + 0.5 * values * (1.0 - tanh_val * tanh_val) * GELU_COEF * (
        1.0 + 3.0 * GELU_CUBE * values * values
    )
    return (value, slope)


def adam_update(weight, mom, var, grad, decay):
    mom_new = BETA_ONE * mom + (1.0 - BETA_ONE) * grad
    var_new = BETA_TWO * var + (1.0 - BETA_TWO) * grad * grad
    fix_one = 1.0 - BETA_ONE**ADAM_STEP
    fix_two = 1.0 - BETA_TWO**ADAM_STEP
    direction = mom_new / fix_one / (jnp.sqrt(var_new / fix_two) + ADAM_EPS)
    return (weight - LEARN * (direction + decay * weight), mom_new, var_new)


def rotated(value, axis, by):
    size = lax.axis_size(axis)
    return lax.ppermute(value, axis, [(i, (i + by) % size) for i in range(size)])


def shifted(value, by):
    size = lax.axis_size(DP)
    return lax.ppermute(
        value, DP, [(i, i + by) for i in range(size) if 0 <= i + by < size]
    )


def pick(value, index):
    return lax.dynamic_index_in_dim(value, index, 0, keepdims=False)


def gather_axis(value, axis):
    size = lax.axis_size(axis)
    me = lax.axis_index(axis)
    if size == 2:
        other = rotated(value, axis, 1)
        return jnp.stack([jnp.where(me == 0, value, other), jnp.where(me == 0, other, value)])
    whole = jnp.zeros((size,) + value.shape, value.dtype)
    whole = lax.dynamic_update_index_in_dim(whole, value, me, 0)
    for by in range(1, size):
        whole = lax.dynamic_update_index_in_dim(
            whole, rotated(value, axis, by), (me - by) % size, 0
        )
    return whole


def scatter_axis(pieces, axis):
    size = lax.axis_size(axis)
    me = lax.axis_index(axis)
    total = pick(pieces, me).astype(fl)
    for by in range(1, size):
        sent = pick(pieces, (me + by) % size).astype(bf)
        total = total + rotated(sent, axis, by).astype(fl)
    return total


def by_dp_axis(pieces, zs, ys):
    return pieces.reshape((zs, ys) + pieces.shape[1:]).swapaxes(0, 1)


def scatter_model(partial, *gates):
    xs, cs = lax.axis_size("x"), lax.axis_size("c")
    rows, width = partial.shape
    view = partial.reshape(xs, cs, rows // (xs * cs), width)
    half = after(scatter_axis(view.swapaxes(0, 1), "c"), *gates)
    return scatter_axis(half, "x")


def gather_model(part, *gates):
    return gather_core(after(gather_axis(part, "x"), *gates))


def gather_core(both):
    four = gather_axis(both, "c").swapaxes(0, 1)
    return four.reshape((-1,) + both.shape[2:])


def ring_index(index, size):
    return index ^ (index >> 1) if size == 4 else index


def ring_step(value):
    size = lax.axis_size("z")
    pairs = [(ring_index(i, size), ring_index((i + 1) % size, size)) for i in range(size)]
    return lax.ppermute(value, "z", pairs)


def ring_source(back):
    size = lax.axis_size("z")
    place = ring_index(lax.axis_index("z"), size)
    return ring_index((place - back + size) % size, size)


def after(value, *others):
    return lax.optimization_barrier((value,) + others)[0]


def over_y(value):
    return [rotated(value, "y", by) for by in range(1, lax.axis_size("y"))]


def in_order(blocks):
    zs, ys = lax.axis_size("z"), lax.axis_size("y")
    me = lax.axis_index("y")
    whole = jnp.zeros((zs * ys,) + blocks[0][0].shape, blocks[0][0].dtype)
    for step, row in enumerate(blocks):
        source = ring_source(step)
        for by, piece in enumerate(row):
            whole = lax.dynamic_update_index_in_dim(
                whole, piece, source * ys + (me - by) % ys, 0
            )
    return whole


TILE = 896
NOMINAL = pl.CostEstimate(flops=1, bytes_accessed=1, transcendentals=0)


def _columns(block, index, valid):
    at = index * TILE + lax.broadcasted_iota(jnp.int32, block.shape, 1)
    return jnp.where(at < valid, block, jnp.zeros_like(block))


def _flat(block):
    return block.reshape(-1, block.shape[-1])


def _hidden_kernel(valid, mid_ref, w_ref, hid_ref, gate_ref, up_ref):
    mid = mid_ref[...]
    gate = jnp.dot(mid, _flat(w_ref[:, 0]), preferred_element_type=fl)
    up = jnp.dot(mid, _flat(w_ref[:, 1]), preferred_element_type=fl)
    value, slope = gelu_parts(gate)
    hid_ref[...] = (value * up).astype(bf)
    gate_ref[...] = (up * slope).astype(bf)
    up_ref[...] = value.astype(bf)


def _down_kernel(valid, hid_ref, down_ref, out_ref):
    index = pl.program_id(0)

    def add(hid, down):
        part = lax.dot_general(hid, down, (((1,), (1,)), ((), ())), preferred_element_type=fl)

        @pl.when(index == 0)
        def _():
            out_ref[...] = part

        @pl.when(index > 0)
        def _():
            out_ref[...] += part

    last = index == pl.num_programs(0) - 1

    @pl.when(jnp.logical_not(last))
    def _():
        add(hid_ref[...], _flat(down_ref[:, 0]))

    @pl.when(last)
    def _():
        add(_columns(hid_ref[...], index, valid), _columns(_flat(down_ref[:, 0]), index, valid))


def _backward_kernel(valid, ffn_ref, gate_ref, up_ref, w_ref, down_ref, mid_ref, ggate_ref, gup_ref):
    index = pl.program_id(0)
    grad = jnp.dot(ffn_ref[...], _flat(down_ref[:, 0]), preferred_element_type=fl)
    ggate = (grad * gate_ref[...].astype(fl)).astype(bf)
    gup = (grad * up_ref[...].astype(fl)).astype(bf)
    ggate_ref[...] = ggate
    gup_ref[...] = gup

    def add(one, two, w_one, w_two):
        dims = (((1,), (1,)), ((), ()))
        part = lax.dot_general(one, w_one, dims, preferred_element_type=fl)
        part = part + lax.dot_general(two, w_two, dims, preferred_element_type=fl)

        @pl.when(index == 0)
        def _():
            mid_ref[...] = part

        @pl.when(index > 0)
        def _():
            mid_ref[...] += part

    last = index == pl.num_programs(0) - 1
    w_one, w_two = _flat(w_ref[:, 0]), _flat(w_ref[:, 1])

    @pl.when(jnp.logical_not(last))
    def _():
        add(ggate, gup, w_one, w_two)

    @pl.when(last)
    def _():
        add(
            _columns(ggate, index, valid),
            _columns(gup, index, valid),
            _columns(w_one, index, valid),
            _columns(w_two, index, valid),
        )


def _grads_kernel(pairs, left_ref, *refs):
    turned = refs[-1]

    @pl.when(pl.program_id(0) == 0)
    def _():
        turned[...] = left_ref[...].T

    for right_ref, out_ref in zip(refs[:pairs], refs[pairs : 2 * pairs]):
        grads = jnp.dot(turned[...], right_ref[...], preferred_element_type=fl).astype(bf)
        out_ref[...] = grads.reshape(out_ref.shape)


def grads_call(left, rights, pieces, name):
    rows, depth = left.shape
    units = rights[0].shape[1]
    split = pieces if depth // pieces % 16 == 0 else 1
    shape = (split, depth // split, units)
    column = pl.BlockSpec((rows, TILE), lambda j: (0, j))
    out = pl.BlockSpec(shape[:2] + (TILE,), lambda j: (0, 0, j))
    results = pl.pallas_call(
        functools.partial(_grads_kernel, len(rights)),
        out_shape=[jax.ShapeDtypeStruct(shape, bf)] * len(rights),
        grid=(pl.cdiv(units, TILE),),
        in_specs=[pl.BlockSpec((rows, depth), lambda j: (0, 0))] + [column] * len(rights),
        out_specs=[out] * len(rights),
        scratch_shapes=[pltpu.VMEM((depth, rows), bf)],
        compiler_params=pltpu.CompilerParams(
            dimension_semantics=("arbitrary",), vmem_limit_bytes=40 * 1024 * 1024
        ),
        cost_estimate=NOMINAL,
        name=name,
    )(left, *rights)
    return [result.reshape(pieces, depth // pieces, units) for result in results]


def ffn_call(kernel, name, rows, lefts, weights, tiles_in, total, tiles_out):
    units = weights[0].shape[-1]
    depth = weights[0].shape[0] * weights[0].shape[2]
    kinds = sum(w.shape[1] for w in weights)
    column = pl.BlockSpec((rows, TILE), lambda j: (0, j))
    whole = pl.BlockSpec((rows, depth), lambda j: (0, 0))
    tile = jax.ShapeDtypeStruct((rows, units), bf)
    return pl.pallas_call(
        functools.partial(kernel, units),
        out_shape=[jax.ShapeDtypeStruct((rows, depth), fl)] * total + [tile] * tiles_out,
        grid=(pl.cdiv(units, TILE),),
        in_specs=[whole] * len(lefts)
        + [column] * len(tiles_in)
        + [pl.BlockSpec(w.shape[:3] + (TILE,), lambda j: (0, 0, 0, j)) for w in weights],
        out_specs=[whole] * total + [column] * tiles_out,
        compiler_params=pltpu.CompilerParams(
            dimension_semantics=("arbitrary",), vmem_limit_bytes=40 * 1024 * 1024
        ),
        cost_estimate=NOMINAL,
        name=name,
    )(*lefts, *tiles_in, *weights)


HALVES = 1


def row_call(kernel, name, rows, by_rows, whole, out_rows, out_whole=(), scratch=()):
    step = rows // HALVES

    def cut(shape):
        return pl.BlockSpec((step,) + shape[1:], lambda i: (i, 0))

    def kept(shape):
        return pl.BlockSpec(shape, lambda i: (0,) * len(shape))

    return pl.pallas_call(
        kernel,
        out_shape=[jax.ShapeDtypeStruct(*item) for item in list(out_rows) + list(out_whole)],
        grid=(HALVES,),
        in_specs=[cut(item.shape) for item in by_rows] + [kept(item.shape) for item in whole],
        out_specs=[cut(item[0]) for item in out_rows] + [kept(item[0]) for item in out_whole],
        scratch_shapes=scratch,
        compiler_params=pltpu.CompilerParams(
            dimension_semantics=("arbitrary",), vmem_limit_bytes=48 * 1024 * 1024
        ),
        cost_estimate=NOMINAL,
        name=name,
    )(*by_rows, *whole)


def _project_kernel(
    x_ref,
    cos_ref,
    sin_ref,
    gain_ref,
    head_ref,
    query_ref,
    keyval_ref,
    normed_ref,
    scale_ref,
    qraw_ref,
    qscale_ref,
    qrot_ref,
    kraw_ref,
    kscale_ref,
    kv_ref,
):
    width = qraw_ref.shape[1]
    values = x_ref[...]
    scale = rms_scale(values)
    scale_ref[...] = scale
    normed = (values * scale * gain_ref[...]).astype(bf)
    normed_ref[...] = normed
    cosine, sine = cos_ref[...], sin_ref[...]

    def turned(raw, scale, factor):
        norm = raw * scale * factor
        return (norm * cosine + rotate_half(norm) * sine).astype(bf)

    raw = jnp.dot(normed, query_ref[...], preferred_element_type=fl)
    scale = rms_scale(raw)
    qraw_ref[...] = raw
    qscale_ref[...] = scale
    qrot_ref[...] = turned(raw, scale, head_ref[0:1])
    raw = jnp.dot(normed, keyval_ref[...], preferred_element_type=fl)
    key = raw[:, :width]
    scale = rms_scale(key)
    kraw_ref[...] = key
    kscale_ref[...] = scale
    kv_ref[:, :width] = turned(key, scale, head_ref[1:2])
    kv_ref[:, width:] = raw[:, width:].astype(bf)


ACROSS = (((1,), (1,)), ((), ()))


def _masked_scores(query, keys, low, high, factor):
    scores = lax.dot_general(query, keys, ACROSS, preferred_element_type=fl) * factor
    at = lax.broadcasted_iota(jnp.int32, scores.shape, 1)
    return jnp.where((at >= low) & (at <= high), scores, NEG_FILL)


def _attend_kernel(
    factor, query_ref, low_ref, high_ref, window_ref, out_ref, att_ref, log_ref, part_ref
):
    width = query_ref.shape[1]
    masked = _masked_scores(
        query_ref[...], window_ref[:, :width], low_ref[...], high_ref[...], factor
    )
    top = jnp.max(masked, axis=-1, keepdims=True)
    powers = jnp.exp(masked - top)
    total = jnp.sum(powers, axis=-1, keepdims=True)
    log_ref[...] = top + jnp.log(total)
    probs = (powers * (1.0 / total)).astype(bf)
    attended = jnp.dot(probs, window_ref[:, width:], preferred_element_type=fl).astype(bf)
    att_ref[...] = attended
    part_ref[...] = lax.dot_general(attended, out_ref[...], ACROSS, preferred_element_type=fl)


def _attend_back_kernel(
    factor,
    grad_ref,
    query_ref,
    low_ref,
    high_ref,
    log_ref,
    att_ref,
    qraw_ref,
    qscale_ref,
    cos_ref,
    sin_ref,
    head_ref,
    window_ref,
    out_ref,
    lowq_ref,
    gqin_ref,
    part_ref,
    gkv_ref,
    ghead_ref,
    turned,
):
    width = query_ref.shape[1]
    keys, values = window_ref[:, :width], window_ref[:, width:]
    query = query_ref[...]
    grad_att = jnp.dot(grad_ref[...], out_ref[...], preferred_element_type=fl).astype(bf)
    delta = jnp.sum(
        grad_att.astype(fl) * att_ref[...].astype(fl), axis=-1, keepdims=True
    )
    masked = _masked_scores(query, keys, low_ref[...], high_ref[...], factor)
    probs = jnp.exp(masked - log_ref[...])
    grad_probs = lax.dot_general(grad_att, values, ACROSS, preferred_element_type=fl)
    grad_scores = (probs * (grad_probs - delta) * factor).astype(bf)
    grad_q = jnp.dot(grad_scores, keys, preferred_element_type=fl)
    grad_k = jnp.dot(query.T, grad_scores, preferred_element_type=fl)
    grad_v = jnp.dot(grad_att.T, probs.astype(bf), preferred_element_type=fl)
    back = grad_q * cos_ref[...] - rotate_half(grad_q * sin_ref[...])
    raw, scale = qraw_ref[...], qscale_ref[...]
    gqin = norm_back(raw, scale, head_ref[0:1], back).astype(bf)
    gqin_ref[...] = gqin
    part_ref[...] = lax.dot_general(gqin, lowq_ref[...], ACROSS, preferred_element_type=fl)
    ghead = jnp.sum(back * raw * scale, axis=0, keepdims=True)
    first = pl.program_id(0) == 0

    @pl.when(first)
    def _():
        turned[:width] = grad_k
        turned[width:] = grad_v
        ghead_ref[...] = ghead

    @pl.when(jnp.logical_not(first))
    def _():
        turned[:width] += grad_k
        turned[width:] += grad_v
        ghead_ref[...] += ghead

    @pl.when(pl.program_id(0) == pl.num_programs(0) - 1)
    def _():
        gkv_ref[...] = turned[...].astype(bf).T


def whole_call(kernel, name, ins, outs):
    def kept(shape):
        return pl.BlockSpec(shape, lambda i: (0,) * len(shape))

    return pl.pallas_call(
        kernel,
        out_shape=[jax.ShapeDtypeStruct(*item) for item in outs],
        grid=(1,),
        in_specs=[kept(item.shape) for item in ins],
        out_specs=[kept(item[0]) for item in outs],
        compiler_params=pltpu.CompilerParams(
            dimension_semantics=("arbitrary",), vmem_limit_bytes=48 * 1024 * 1024
        ),
        cost_estimate=NOMINAL,
        name=name,
    )(*ins)


def _input_back_kernel(parts, *refs):
    cos_ref, sin_ref, raw_ref, scale_ref, head_ref, low_ref = refs[parts : parts + 6]
    (
        normed_ref,
        in_ref,
        scale_in_ref,
        resid_grad_ref,
        attn_ref,
        scale_attn_ref,
        mid_grad_ref,
        resid_ref,
        scale_mid_ref,
        out_grad_ref,
        ffn_ref,
        scale_ffn_ref,
        gain_ref,
        gkv_ref,
        ghead_ref,
        grad_ref,
        layers_ref,
    ) = refs[parts + 6 :]
    width = raw_ref.shape[1]
    total = refs[0][...]
    for ref in refs[1:parts]:
        total = total + ref[...].astype(fl)
    grad = total[:, :width]
    back = grad * cos_ref[...] - rotate_half(grad * sin_ref[...])
    raw, scale = raw_ref[...], scale_ref[...]
    gkv_ref[:, :width] = norm_back(raw, scale, head_ref[1:2], back).astype(bf)
    gkv_ref[:, width:] = total[:, width:].astype(bf)
    ghead_ref[...] = jnp.sum(back * raw * scale, axis=0, keepdims=True)
    part = lax.dot_general(gkv_ref[...], low_ref[...], ACROSS, preferred_element_type=fl)
    normed = normed_ref[...] + part
    values, scale, resid_grad = in_ref[...], scale_in_ref[...], resid_grad_ref[...]
    grad_ref[...] = (resid_grad + norm_back(values, scale, gain_ref[0:1], normed)).astype(bf)

    def over_rows(item):
        return jnp.sum(item, axis=0, keepdims=True)

    layers_ref[0:1] = over_rows(normed * values * scale)
    layers_ref[1:2] = over_rows(resid_grad * attn_ref[...] * scale_attn_ref[...])
    layers_ref[2:3] = over_rows(mid_grad_ref[...] * resid_ref[...] * scale_mid_ref[...])
    layers_ref[3:4] = over_rows(out_grad_ref[...] * ffn_ref[...] * scale_ffn_ref[...])


def on_device(
    block_in,
    out_grad,
    segment_ids,
    w_query,
    w_keyval,
    w_out,
    w_gateup,
    w_down,
    gain_layers,
    gain_heads,
    mom_query,
    var_query,
    mom_keyval,
    var_keyval,
    mom_out,
    var_out,
    mom_gateup,
    var_gateup,
    mom_down,
    var_down,
    mom_layers,
    var_layers,
    mom_heads,
    var_heads,
):
    zs, ys = lax.axis_size("z"), lax.axis_size("y")
    xs, cs = lax.axis_size("x"), lax.axis_size("c")
    dps, mps = zs * ys, xs * cs
    model = lax.axis_index("x") * cs + lax.axis_index("c")
    device = lax.axis_index("z") * ys + lax.axis_index("y")
    width = HD
    rows, depth = block_in.shape
    quarter = rows // mps
    factor = width ** (-0.5)
    norm_factor = float(rows * dps) ** (-0.5)
    drows = w_query.shape[0]
    krows = w_keyval.shape[0]
    gcols, hcols = gain_layers.shape[1], gain_heads.shape[1]

    kpad = -(-krows // 16) * 16
    small = jnp.concatenate([gain_layers.reshape(-1), gain_heads.reshape(-1)]).astype(bf)
    small = jnp.pad(small, (0, width - small.shape[0])).reshape(1, width)
    fill = jnp.zeros((kpad - krows, width), bf)
    pack = jnp.concatenate(
        [
            w_query.astype(bf),
            w_keyval[:, :width].astype(bf),
            fill,
            w_keyval[:, width:].astype(bf),
            fill,
            jnp.pad(small, ((0, 15), (0, 0))),
        ],
        axis=0,
    )
    by_z = gather_axis(pack, "z")
    by_dp = gather_axis(by_z, "y").swapaxes(0, 1).reshape((dps,) + pack.shape)
    low_query = by_dp[:, :drows].reshape(depth, width)
    kv_mine = by_dp[:, drows:]

    gateup0, down0 = w_gateup.astype(bf), w_down.T.astype(bf)
    gateup1 = ring_step(after(gateup0, by_z))
    gateup0_y = over_y(after(gateup0, by_dp))
    gateup2 = ring_step(gateup1)
    gateup1_y = over_y(after(gateup1, *gateup0_y))
    gateup3 = ring_step(gateup2)
    down_y = over_y(after(down0, *gateup1_y))

    kv_all = gather_axis(gather_axis(after(kv_mine, gateup1), "x"), "c")
    kv_all = after(kv_all, gateup2, *gateup0_y)
    lanes = np.arange(cs * xs * dps * kpad).reshape(cs, xs, dps, kpad)
    core, xx, dd, rr = np.unravel_index(lanes.reshape(-1), lanes.shape)
    owner = np.where(rr < krows, (dd * mps + xx * cs + core) * krows + rr, -1)
    depth_index = jnp.arange(depth, dtype=jnp.int32)
    sorter = (depth_index[:, None] == jnp.asarray(owner, jnp.int32)[None, :]).astype(bf)
    kv_pad = jnp.concatenate(
        [
            kv_all[:, :, :, :kpad].reshape(-1, width),
            kv_all[:, :, :, kpad : 2 * kpad].reshape(-1, width),
        ],
        axis=1,
    )
    low_keyval = jnp.dot(sorter, kv_pad, preferred_element_type=fl).astype(bf)
    low_keyval = after(low_keyval, gateup3, *gateup1_y)
    mine = np.arange(dps * kpad)
    owner = (mine // kpad) * mps * krows + mine % kpad
    owner = jnp.asarray(owner, jnp.int32) + model * krows
    chooser = (depth_index[:, None] == owner[None, :]) & jnp.asarray(mine % kpad < krows)[None, :]
    gains = kv_all[:, :, :, 2 * kpad].astype(fl)
    gain_scale = 1.0 + gains[:, :, :, : 4 * gcols].reshape(cs, xs, dps, 4, gcols).transpose(
        3, 2, 1, 0, 4
    ).reshape(4, depth)
    head_scale = 1.0 + gains[:, :, :, 4 * gcols : 4 * gcols + 2 * hcols].reshape(
        cs, xs, dps, 2, hcols
    ).transpose(3, 2, 1, 0, 4).reshape(2, width)

    margin = SEQ // 2
    first_row = device * rows
    shifted_first = first_row + margin
    seq_start = shifted_first // SEQ * SEQ
    span = SEQ // rows
    position = shifted_first + jnp.arange(rows, dtype=jnp.int32)
    cosine, sine = rope_tables(position % SEQ, width)

    def part_rows(values):
        return lax.dynamic_slice_in_dim(values, model * quarter, quarter, 0)

    (
        normed_in,
        scale_in,
        query_raw,
        scale_query,
        query_rot,
        key_raw,
        scale_key,
        keyval_low,
    ) = row_call(
        _project_kernel,
        "project",
        rows,
        [block_in, cosine, sine],
        [gain_scale[0:1], head_scale, low_query, low_keyval],
        [
            ((rows, depth), bf),
            ((rows, 1), fl),
            ((rows, width), fl),
            ((rows, 1), fl),
            ((rows, width), bf),
            ((rows, width), fl),
            ((rows, 1), fl),
            ((rows, 2 * width), bf),
        ],
    )
    sent_kv = after(part_rows(keyval_low), *down_y)
    earlier = jnp.stack([shifted(sent_kv, by) for by in range(span - 1, 0, -1)])
    out_by_z = gather_axis(after(w_out.T.astype(bf), sent_kv), "z")
    low_out = gather_axis(out_by_z, "y").swapaxes(0, 1).reshape(depth, width)
    down0 = after(jnp.stack([down0] + down_y), earlier, out_by_z)
    down1 = ring_step(down0)
    gateup2_y = over_y(after(gateup2, earlier, low_out))
    four = gather_axis(gather_axis(earlier, "x"), "c")
    earlier = four.transpose(2, 1, 0, 3, 4).reshape((span - 1) * rows, 2 * width)
    earlier = after(earlier, down1, *gateup2_y)
    window = jnp.concatenate([earlier, keyval_low], axis=0)
    reach = span * rows
    window_first = first_row + rows - reach
    seg_query = lax.dynamic_slice_in_dim(segment_ids, first_row, rows, 0)
    doc_first = jnp.sum(
        (segment_ids[None, :] < seg_query[:, None]).astype(jnp.int32), axis=1, keepdims=True
    )
    run_first = jnp.maximum(doc_first, seq_start - margin) - window_first
    run_last = jnp.arange(rows, dtype=jnp.int32)[:, None] + (reach - rows)
    attended, log_total, attn_part = row_call(
        functools.partial(_attend_kernel, factor),
        "attend",
        rows,
        [query_rot, run_first, run_last],
        [window, low_out],
        [((rows, width), bf), ((rows, 1), fl), ((rows, depth), fl)],
    )
    down2 = ring_step(down1)
    gateup3_y = over_y(after(gateup3, *gateup2_y))

    in_part, scale_in_part = part_rows(block_in), part_rows(scale_in)
    grad_part = part_rows(out_grad)
    attn_proj = after(scatter_model(attn_part), down2, *gateup3_y)
    down3 = ring_step(down2)
    scale_attn = rms_scale(attn_proj)
    resid = in_part + attn_proj * scale_attn * gain_scale[1]
    scale_mid = rms_scale(resid)
    normed_mid = gather_model((resid * scale_mid * gain_scale[2]).astype(bf))
    low_gateup = in_order(
        [
            [gateup0] + gateup0_y,
            [gateup1] + gateup1_y,
            [gateup2] + gateup2_y,
            [gateup3] + gateup3_y,
        ]
    )
    low_down = in_order([[block[by] for by in range(ys)] for block in (down0, down1, down2, down3)])
    low_down = low_down[:, None]
    if drows % 16:
        low_gateup = low_gateup.swapaxes(0, 1).reshape((1, 2, depth, -1))
        low_down = low_down.reshape((1, 1, depth, -1))
    hidden, gate_factor, up_factor = ffn_call(
        _hidden_kernel, "ffn_hidden", rows, [normed_mid], [low_gateup], [], 0, 3
    )
    (ffn_part,) = ffn_call(_down_kernel, "ffn_down", rows, [], [low_down], [hidden], 1, 0)
    ffn_proj = scatter_model(ffn_part)
    scale_ffn = rms_scale(ffn_proj)
    grad_ffn = gather_model(norm_back(ffn_proj, scale_ffn, gain_scale[3], grad_part).astype(bf))
    (grad_down,) = grads_call(grad_ffn, [hidden], dps, "down_grads")
    grad_down = grad_down.reshape((zs, ys) + grad_down.shape[1:])
    sum_down1 = ring_step(pick(grad_down, ring_source(1)))
    grad_ffn = after(grad_ffn, grad_down)
    mid_part, grad_gate, grad_up = ffn_call(
        _backward_kernel,
        "ffn_backward",
        rows,
        [grad_ffn],
        [low_gateup, low_down],
        [gate_factor, up_factor],
        1,
        2,
    )
    mid_part = after(mid_part, sum_down1)
    grads_gateup = grads_call(normed_mid, [grad_gate, grad_up], dps, "gateup_grads")

    def gateup_piece(target, by):
        index = ring_source(target) * ys + (lax.axis_index("y") + by) % ys
        return jnp.stack([pick(item, index) for item in grads_gateup])

    def gateup_over_y(target, *gates):
        return [
            rotated(after(gateup_piece(target, by), *gates), "y", by) for by in range(1, ys)
        ]

    def gateup_add(came, target, over):
        total = gateup_piece(target, 0).astype(fl)
        for item in ([] if came is None else [came]) + over:
            total = total + item.astype(fl)
        return total

    def down_add(came, target):
        return came.astype(fl) + pick(grad_down, ring_source(target)).astype(fl)

    over_a = gateup_over_y(1)
    over_b = gateup_over_y(2, *over_a)
    down_two = down_add(sum_down1, 2).astype(bf)
    sum_down2 = ring_step(down_two)
    grad_mid = after(scatter_model(mid_part, down_two), sum_down2, *over_a)
    down_three = down_add(sum_down2, 3).astype(bf)
    sum_down3 = ring_step(down_three)
    grad_resid = grad_part + norm_back(resid, scale_mid, gain_scale[2], grad_mid)
    grad_attn = gather_axis(
        norm_back(attn_proj, scale_attn, gain_scale[1], grad_resid).astype(bf), "x"
    )
    grad_attn = gather_core(after(grad_attn, sum_down3, *over_b))
    gateup_one = gateup_add(None, 1, [after(item, sum_down3) for item in over_a]).astype(bf)
    sum_gateup1 = ring_step(gateup_one)
    over_c = gateup_over_y(3, *over_b)
    grad_attn = after(grad_attn, gateup_one)
    grad_out = jnp.einsum("td,tc->dc", grad_attn, attended, preferred_element_type=fl)
    grad_qin, normed_part, grad_seq, grad_qhead = row_call(
        functools.partial(_attend_back_kernel, factor),
        "attend_back",
        rows,
        [
            grad_attn,
            query_rot,
            run_first,
            run_last,
            log_total,
            attended,
            query_raw,
            scale_query,
            cosine,
            sine,
        ],
        [head_scale, window, low_out, low_query],
        [((rows, width), bf), ((rows, depth), fl)],
        [((reach, 2 * width), bf), ((1, width), fl)],
        [pltpu.VMEM((2 * width, reach), fl)],
    )
    grad_query = jnp.einsum("td,tc->dc", normed_in, grad_qin, preferred_element_type=fl)
    grad_qo = jnp.concatenate(
        [
            grad_query.reshape(dps, drows, width).astype(bf),
            grad_out.reshape(dps, drows, width).astype(bf),
        ],
        axis=1,
    )
    qo_over_y = scatter_axis(by_dp_axis(after(grad_qo, *over_c), zs, ys), "y").astype(bf)
    grad_seq = after(grad_seq, sum_gateup1, *over_c)
    gateup_two = gateup_add(sum_gateup1, 2, over_b).astype(bf)
    sum_gateup2 = ring_step(gateup_two)
    by_model = grad_seq.reshape(span, xs, cs, quarter, 2 * width).transpose(2, 1, 0, 3, 4)
    over_d = gateup_over_y(4, qo_over_y)
    by_block = after(scatter_axis(by_model, "c"), gateup_two)
    own, own_z = lax.axis_index("y"), lax.axis_index("z")
    qo_over_z = [
        rotated(pick(qo_over_y, (own_z + by) % zs), "z", by) for by in range(1, zs)
    ]
    by_block = after(scatter_axis(by_block, "x"), sum_gateup2, *over_d, *qo_over_z)
    grad_kparts = [by_block[span - 1]] + [
        shifted(by_block[span - 1 - by].astype(bf), -by) for by in range(1, span)
    ]
    gateup_three = gateup_add(after(sum_gateup2, *grad_kparts), 3, over_c).astype(bf)
    gateup_three = [gateup_three[i] for i in range(2)]
    sum_gateup3 = [ring_step(gateup_three[0])]
    sum_gateup3.append(ring_step(after(gateup_three[1], *sum_gateup3)))
    grad_kparts[0] = after(grad_kparts[0], *gateup_three)

    sum_down = down_add(after(sum_down3, by_block), 4)
    down_over_y = [
        rotated(after(pick(sum_down, (own + by) % ys).astype(bf), *grad_kparts), "y", by)
        for by in range(1, ys)
    ]

    ffn_late = after(ffn_proj, grad_seq)
    out_part = (resid + ffn_late * scale_ffn * gain_scale[3]).astype(bf)
    block_out = gather_model(after(out_part, by_block)).astype(fl)

    cos_part, sin_part = part_rows(cosine), part_rows(sine)
    key_part, scale_kpart = part_rows(key_raw), part_rows(scale_key)
    grad_kvin, grad_khead, grad_in_part, grad_layers = whole_call(
        functools.partial(_input_back_kernel, span),
        "input_back",
        grad_kparts
        + [cos_part, sin_part, key_part, scale_kpart, head_scale, low_keyval]
        + [
            scatter_model(normed_part),
            in_part,
            scale_in_part,
            grad_resid,
            attn_proj,
            scale_attn,
            grad_mid,
            resid,
            scale_mid,
            grad_part,
            ffn_proj,
            scale_ffn,
            gain_scale,
        ],
        [((quarter, 2 * width), bf), ((1, width), fl), ((quarter, depth), bf), ((4, depth), fl)],
    )
    normed_mine = jnp.dot(after(normed_in, grad_seq), chooser.astype(bf), preferred_element_type=fl).astype(bf)
    grad_keyval = jnp.einsum(
        "td,tc->dc", normed_mine, gather_model(grad_kvin, sum_gateup3[0], *down_over_y), preferred_element_type=fl
    ).reshape(dps, kpad, 2 * width)

    grad_input = gather_model(grad_in_part).astype(fl)
    grad_heads = jnp.concatenate([grad_qhead, grad_khead], axis=0)
    grad_small = jnp.concatenate(
        [
            grad_layers.reshape(4, dps, mps, gcols).transpose(1, 2, 0, 3).reshape(dps, mps, -1),
            grad_heads.reshape(2, dps, mps, hcols).transpose(1, 2, 0, 3).reshape(dps, mps, -1),
        ],
        axis=2,
    )
    grad_small = jnp.pad(grad_small, ((0, 0), (0, 0), (0, width - grad_small.shape[2])))
    grad_small = grad_small.reshape(dps, xs, cs, width).transpose(2, 1, 0, 3)
    grad_small = scatter_axis(scatter_axis(grad_small, "c"), "x")
    grad_pack = jnp.concatenate(
        [
            grad_keyval[:, :, :width].astype(bf),
            grad_keyval[:, :, width:].astype(bf),
            jnp.pad(grad_small[:, None].astype(bf), ((0, 0), (0, 15), (0, 0))),
        ],
        axis=1,
    )
    sums_pack = scatter_axis(by_dp_axis(grad_pack, zs, ys), "y")
    sums_pack = scatter_axis(after(sums_pack, sum_gateup3[1]), "z")
    sums_qo = pick(after(qo_over_y, grad_pack), own_z).astype(fl)
    for item in qo_over_z:
        sums_qo = sums_qo + item.astype(fl)
    sum_query, sum_out = sums_qo[:drows], sums_qo[drows:].T
    sum_gateup = gateup_add(after(jnp.stack(sum_gateup3), grad_pack), 4, over_d)
    sum_down = pick(after(sum_down, grad_pack), own)
    for item in down_over_y:
        sum_down = sum_down + item.astype(fl)
    sum_down = sum_down.T
    sum_keyval = jnp.concatenate([sums_pack[:krows], sums_pack[kpad : kpad + krows]], axis=1)
    sum_small = sums_pack[2 * kpad]
    sum_layers = sum_small[: 4 * gcols].reshape(4, gcols)
    sum_heads = sum_small[4 * gcols : 4 * gcols + 2 * hcols].reshape(2, hcols)

    masters = (w_query, w_keyval, w_out, w_gateup, w_down, gain_layers, gain_heads)
    sums = (sum_query, sum_keyval, sum_out, sum_gateup, sum_down, sum_layers, sum_heads)
    totals = tuple((item * norm_factor for item in sums))
    moms = (mom_query, mom_keyval, mom_out, mom_gateup, mom_down, mom_layers, mom_heads)
    varis = (var_query, var_keyval, var_out, var_gateup, var_down, var_layers, var_heads)
    decays = (DECAY, DECAY, DECAY, DECAY, DECAY, 0.0, 0.0)
    updated = [
        adam_update(master, mom, var, grad, decay)
        for master, mom, var, grad, decay in zip(masters, moms, varis, totals, decays)
    ]
    return (
        (block_out, grad_input)
        + totals
        + tuple(item[0] for item in updated)
        + tuple(item[1] for item in updated)
        + tuple(item[2] for item in updated)
    )


def solution(mesh):
    dps, mps = mesh.shape["dp"], mesh.shape["mp"]
    zs = 4 if dps % 4 == 0 else 1
    cs = 2 if mps % 2 == 0 else 1
    split = Mesh(mesh.devices.reshape(zs, dps // zs, mps // cs, cs), ("z", "y", "x", "c"))
    mp = ("x", "c")
    both = DP + mp
    weights = (
        P(DP, mp),
        P(both, None),
        P(mp, DP),
        P(None, DP, mp),
        P(mp, DP),
        P(None, both),
        P(None, both),
    )
    tokens = P(DP, None)
    states = tuple(spec for spec in weights for _ in range(2))
    in_specs = (tokens, tokens, P()) + weights + states
    out_specs = (tokens, tokens) + weights * 4
    return jax.shard_map(
        on_device, mesh=split, in_specs=in_specs, out_specs=out_specs, check_vma=False
    )
```
